512 devices in a mesh: aux: 32 (over x_hi, z), occ: 4 (over y), vir: 4 (over x_lo, core).
Axes of the slice: x: 4 (x_hi: 2, x_lo: 2; x = x_hi * 2 + x_lo), y: 4, z: 16, core: 2. Of those that a mesh axis runs over, the one named last changes fastest.
Arguments:
- start_block: float32 [8, 80, 512], P(None, 'occ', 'vir'), may hold values from -6 to 6
- factors: bfloat16 [2, 8192, 80, 512], P(None, 'aux', 'occ', 'vir'), may hold values from -0.0625 to 0.0625
- eps_occ: float32 [80], P('occ'), may hold values from -1.2 to -0.3
- eps_vir: float32 [512], P('vir'), may hold values from 0.1 to 1.5
Outputs:
- coefficients: float32 [4, 8, 8], replicated
- next_block: float32 [8, 80, 512], P(None, 'occ', 'vir')
The draws below stay inside these ranges and needn't reach their ends.
All inputs are finite; a program needn't handle non-finite values.
Results may differ from the reference program's by a relative error of at most 0.007.
Values sent between devices are 32-bit elements; how exact they have to be, the bound alone decides.
A program may use at most 64 MiB of HBM per device.

```python
import jax
import jax.numpy as jnp
from jax import lax

NV = 8
OCC = 80
VIR = 512
AUX = 8192


def level_of(rng, dims, shards, smallest, high):
    loudness, own = 1.0, jax.random.fold_in(rng, 6)
    for position, blocks in shards:
        heights = jnp.exp(jax.random.uniform(jax.random.fold_in(own, position), (blocks,), jnp.float32, smallest / len(shards), high / len(shards)))
        loudness = loudness * jnp.repeat(heights, dims[position] // blocks).reshape([-1 if axis == position else 1 for axis in range(len(dims))])
    return loudness


def centred(own_key, extent, deviation, most, pieces=(), held_as=jnp.bfloat16):
    array = jax.random.normal(own_key, extent, jnp.float32) * deviation
    if len(pieces) > 0:
        array = level_of(own_key, extent, pieces, -0.22, 0.18) * array
    return jnp.clip(array, min=-most, max=most).astype(held_as)


def setup_inputs(seed: int = 0) -> dict:
    seeds = jax.random.split(jax.random.key(seed), 5)
    return {
        "start_block": centred(seeds[0], (NV, OCC, VIR), 1.0, 6.0, ((1, 4), (2, 4)), jnp.float32),
        "factors": centred(seeds[1], (2, AUX, OCC, VIR), (OCC * VIR // 4) ** -0.5, 0.0625, ((1, 32), (2, 4), (3, 4))),
        "eps_occ": jnp.clip(-1.2 + 0.90000004 * jax.random.uniform(seeds[2], (OCC,), jnp.float32) ** level_of(seeds[2], (OCC,), ((0, 4),), -0.2, 0.2), -1.2, -0.3),
        "eps_vir": jnp.clip(0.1 + 1.4 * jax.random.uniform(seeds[3], (VIR,), jnp.float32) ** level_of(seeds[3], (VIR,), ((0, 4),), -0.2, 0.2), 0.1, 1.5),
    }


def precise(left, right):
    return jnp.dot(left.astype(jnp.float32), right.astype(jnp.float32), precision=lax.Precision.HIGHEST, preferred_element_type=jnp.float32)

def orthonormal(gram, block):
    lower = jnp.linalg.cholesky(gram)
    eye_mat = jnp.eye(gram.shape[0], dtype=jnp.float32)
    inverse = lax.linalg.triangular_solve(lower, eye_mat, left_side=True, lower=True)
    return (lower, precise(inverse, block))

def reference(start_block, factors, eps_occ, eps_vir):
    total = OCC * VIR
    delta = (eps_vir[None, :] - eps_occ[:, None]).reshape(1, total)
    flat = factors.reshape(2, AUX, total)
    block = start_block.reshape(NV, total)
    gram = precise(block, block.T) / total
    lower, current = orthonormal(gram, block)
    previous = None
    coeffs = []
    for step in range(2):
        low = current.astype(jnp.bfloat16)
        bare = (2.0 * jnp.dot(low.astype(jnp.float32), flat[0].T.astype(jnp.float32), preferred_element_type=jnp.float32)).astype(jnp.bfloat16)
        screen = (-1.0 * jnp.dot(low.astype(jnp.float32), flat[1].T.astype(jnp.float32), preferred_element_type=jnp.float32)).astype(jnp.bfloat16)
        image = delta * current + jnp.dot(bare.astype(jnp.float32), flat[0].astype(jnp.float32), preferred_element_type=jnp.float32) + jnp.dot(screen.astype(jnp.float32), flat[1].astype(jnp.float32), preferred_element_type=jnp.float32)
        proj = precise(image, current.T) / total
        resid = image - precise(proj, current)
        if previous is not None:
            cross = precise(image, previous.T) / total
            resid = resid - precise(cross, previous)
        rgram = precise(resid, resid.T) / total
        lower, following = orthonormal(rgram, resid)
        coeffs.append(proj)
        coeffs.append(lower.T)
        previous = current
        current = following
    return (jnp.stack(coeffs), current.reshape(NV, OCC, VIR))
```

```python
import jax
import jax.numpy as jnp
from jax import lax
from jax.experimental import pallas as pl
from jax.experimental.pallas import tpu as pltpu
from jax.sharding import PartitionSpec as P

AUX_WAYS, OCC_WAYS, VIR_WAYS = 32, 4, 4
NV, ROWS, LANES, DEPTH = 8, 20, 128, 256
PAIRS = 40960
TILES = ROWS + 1
STRIDE, UNSTRIDE = 3, 11
GROUP = 4
MESH = pl.DeviceIdType.MESH
f32, bf16 = jnp.float32, jnp.bfloat16


def split(value):
    high = value.astype(bf16)
    low = (value - high.astype(f32)).astype(bf16)
    return jnp.concatenate([high, low], axis=0)


def merge(value):
    return value[:NV] + value[NV:]


def apply(matrix, value, first=0):
    total = matrix[:, first:first + 1] * value[0:1, :]
    for m in range(1, NV):
        total = total + matrix[:, first + m:first + m + 1] * value[m:m + 1, :]
    return total


def iotas():
    return (
        lax.broadcasted_iota(jnp.int32, (NV, LANES), 0),
        lax.broadcasted_iota(jnp.int32, (NV, LANES), 1),
    )


def factor(gram):
    row, lane = iotas()
    work = jnp.where(lane < NV, gram, jnp.where(lane == row + NV, 1.0, 0.0))
    scale = jnp.ones((NV, 1), f32)
    rows1 = lax.broadcasted_iota(jnp.int32, (NV, 1), 0)
    for k in range(NV):
        pivot = work[k:k + 1, k:k + 1]
        scale = jnp.where(rows1 == k, pivot, scale)
        if k < NV - 1:
            ratio = jnp.where(rows1 > k, work[:, k:k + 1] / pivot, 0.0)
            work = work - ratio * work[k:k + 1, :]
    return work * (1.0 / jnp.sqrt(scale))


def columns(sums):
    _, lane = iotas()
    out = jnp.zeros((NV, LANES), f32)
    for m, value in enumerate(sums):
        out = jnp.where(lane == m, jnp.sum(value, axis=1, keepdims=True), out)
    return out


def products(lefts, rights):
    sums = []
    for m in range(NV):
        total = lefts[0] * rights[0][m:m + 1, :]
        for left, right in zip(lefts[1:], rights[1:]):
            total = total + left * right[m:m + 1, :]
        sums.append(total)
    return sums


def kernel(
    start_hbm, fac_hbm, occ_hbm, vir_hbm,
    coef_ref, next_ref,
    start, fac, eocc, evir, q1, q2, r1, xhat,
    cvir, cocc, part, rs, ag, mine, gm,
    in_sem, fac_sem, cv_send, cv_recv, co_send, co_recv,
    rs_send, rs_recv, ag_send, ag_recv, g_send, g_recv,
):
    aux = lax.axis_index("aux")
    occ = lax.axis_index("occ")
    vir = lax.axis_index("vir")
    spot = occ * VIR_WAYS + vir
    tile = lax.rem(aux * UNSTRIDE, AUX_WAYS)
    owner = tile < TILES

    loads = [
        pltpu.make_async_copy(start_hbm, start, in_sem.at[0]),
        pltpu.make_async_copy(occ_hbm, eocc, in_sem.at[1]),
        pltpu.make_async_copy(vir_hbm, evir, in_sem.at[2]),
    ]
    fac_loads = [
        pltpu.make_async_copy(
            fac_hbm.at[:, pl.ds(GROUP * c, GROUP)], fac.at[:, pl.ds(GROUP * c, GROUP)], fac_sem.at[c]
        )
        for c in range(ROWS // GROUP)
    ]
    for load in loads + fac_loads:
        load.start()

    barrier = pltpu.get_barrier_semaphore()

    def greet_aux(d, carry):
        pl.semaphore_signal(
            barrier, inc=1, device_id={"aux": lax.rem(aux + d, AUX_WAYS)}, device_id_type=MESH
        )
        return carry

    def greet_spot(d, carry):
        other = lax.rem(spot + d, OCC_WAYS * VIR_WAYS)
        pl.semaphore_signal(
            barrier, inc=1,
            device_id={"occ": other // VIR_WAYS, "vir": lax.rem(other, VIR_WAYS)}, device_id_type=MESH,
        )
        return carry

    lax.fori_loop(1, AUX_WAYS, greet_aux, 0)
    lax.fori_loop(1, OCC_WAYS * VIR_WAYS, greet_spot, 0)

    for load in loads:
        load.wait()

    def delta(i):
        return evir[...] - eocc[i]

    def contract(source, waits):
        sums = [None, None]
        for i in range(0, ROWS, 2):
            if waits and i % GROUP == 0:
                fac_loads[i // GROUP].wait()
            left = jnp.concatenate([split(source[i]), split(source[i + 1])], axis=1)
            for s in range(2):
                right = jnp.concatenate([fac[s, i], fac[s, i + 1]], axis=1)
                term = lax.dot_general(
                    left, right, (((1,), (1,)), ((), ())), preferred_element_type=f32
                )
                sums[s] = term if sums[s] is None else sums[s] + term
        return [merge(sums[s])[:, LANES * h:LANES * (h + 1)] for s in range(2) for h in range(2)]

    def wait_bytes(ref, sem):
        pltpu.make_async_copy(ref, ref, sem).wait()

    def sum_group(step, tiles, first):
        count = len(tiles)
        for index, value in enumerate(tiles):
            cvir[step, vir, index] = value
        if first:
            pl.semaphore_wait(barrier, AUX_WAYS - 1 + OCC_WAYS * VIR_WAYS - 1)
        for d in range(1, VIR_WAYS):
            pltpu.make_async_remote_copy(
                src_ref=cvir.at[step, vir], dst_ref=cvir.at[step, vir],
                send_sem=cv_send.at[step], recv_sem=cv_recv.at[step],
                device_id={"vir": lax.rem(vir + d, VIR_WAYS)}, device_id_type=MESH,
            ).start()
        wait_bytes(cvir.at[step, pl.ds(0, VIR_WAYS - 1)], cv_recv.at[step])
        for index in range(count):
            cocc[step, occ, index] = (
                (cvir[step, 0, index] + cvir[step, 1, index])
                + (cvir[step, 2, index] + cvir[step, 3, index])
            )
        for d in range(1, OCC_WAYS):
            pltpu.make_async_remote_copy(
                src_ref=cocc.at[step, occ], dst_ref=cocc.at[step, occ],
                send_sem=co_send.at[step], recv_sem=co_recv.at[step],
                device_id={"occ": lax.rem(occ + d, OCC_WAYS)}, device_id_type=MESH,
            ).start()
        wait_bytes(cocc.at[step, pl.ds(0, OCC_WAYS - 1)], co_recv.at[step])
        return [
            (cocc[step, 0, index] + cocc[step, 1, index])
            + (cocc[step, 2, index] + cocc[step, 3, index])
            for index in range(count)
        ]

    def send_tiles(step, first, last):
        def body(t, carry):
            target = lax.rem(t * STRIDE, AUX_WAYS)

            @pl.when(target != aux)
            def _():
                pltpu.make_async_remote_copy(
                    src_ref=part.at[step, t], dst_ref=rs.at[step, aux],
                    send_sem=rs_send.at[step], recv_sem=rs_recv.at[step],
                    device_id={"aux": target}, device_id_type=MESH,
                ).start()

            @pl.when(target == aux)
            def _():
                rs[step, aux] = part[step, t]

            return carry

        lax.fori_loop(first, last, body, 0)

    def back(step, sums):
        scaled = [
            split(jnp.concatenate([2.0 * sums[0], 2.0 * sums[1]], axis=1)),
            split(jnp.concatenate([-sums[2], -sums[3]], axis=1)),
        ]
        for base in range(0, ROWS, GROUP):
            for i in range(base, base + GROUP, 2):
                both = None
                for s in range(2):
                    right = jnp.concatenate([fac[s, i], fac[s, i + 1]], axis=1)
                    term = lax.dot_general(
                        scaled[s], right, (((1,), (0,)), ((), ())), preferred_element_type=f32
                    )
                    both = term if both is None else both + term
                both = merge(both)
                part[step, i] = both[:, :LANES]
                part[step, i + 1] = both[:, LANES:]
            send_tiles(step, base, base + GROUP)

    def spread(step, lower, extra):
        @pl.when(owner)
        def _():
            wait_bytes(rs.at[step, pl.ds(0, AUX_WAYS - 1)], rs_recv.at[step])
            sums = [rs[step, j] for j in range(AUX_WAYS)]
            while len(sums) > 1:
                sums = [a + b for a, b in zip(sums[0::2], sums[1::2])]

            @pl.when(tile < ROWS)
            def _():
                mine[step] = apply(lower, sums[0], NV)

            @pl.when(tile == ROWS)
            def _():
                mine[step] = (sums[0] + extra) * (1.0 / PAIRS)

            def body(d, carry):
                pltpu.make_async_remote_copy(
                    src_ref=mine.at[step], dst_ref=ag.at[step, tile],
                    send_sem=ag_send.at[step], recv_sem=ag_recv.at[step],
                    device_id={"aux": lax.rem(aux + d, AUX_WAYS)}, device_id_type=MESH,
                ).start()
                return carry

            lax.fori_loop(1, AUX_WAYS, body, 0)
            ag[step, tile] = mine[step]
            wait_bytes(ag.at[step, pl.ds(0, TILES - 1)], ag_recv.at[step])

        @pl.when(jnp.logical_not(owner))
        def _():
            wait_bytes(ag.at[step], ag_recv.at[step])

    def small(left, right):
        return lax.dot_general(
            left, right, (((1,), (1,)), ((), ())),
            precision=lax.Precision.HIGHEST, preferred_element_type=f32,
        )

    def wide(value):
        return jnp.concatenate(
            [value, jnp.zeros((value.shape[0], LANES - value.shape[1]), f32)], axis=1
        )

    row, lane = iotas()
    weights = [2.0, 2.0, -1.0, -1.0]

    vecs = [start[i] for i in range(ROWS)]
    shifted = [vecs[i] * delta(i) for i in range(ROWS)]
    grams = columns(products(vecs, vecs) + products(vecs, shifted))
    sums = contract(vecs, True)
    *sums, grams = sum_group(0, sums + [grams], True)
    back(0, sums)
    lower = factor(grams * (1.0 / PAIRS))
    inverse = lower[:, NV:2 * NV]
    hats = [apply(lower, value, NV) for value in sums]
    for index in range(4):
        xhat[index] = hats[index]
    part[0, ROWS] = columns(products([w * hat for w, hat in zip(weights, hats)], hats))
    send_tiles(0, ROWS, TILES)
    middle = small(small(inverse, grams[:, NV:2 * NV]), inverse)
    for i in range(ROWS):
        q1[i] = apply(lower, start[i], NV)
    spread(0, lower, wide(middle))
    proj = ag[0, ROWS]
    coef_ref[0] = proj[:, :NV]
    for i in range(ROWS):
        r1[i] = ag[0, i] + delta(i) * q1[i] - apply(proj, q1[i])

    vecs = [r1[i] for i in range(ROWS)]
    moved = [delta(i) * q1[i] for i in range(ROWS)]
    shifted = [vecs[i] * delta(i) for i in range(ROWS)]
    grams = columns(products(vecs, vecs) + products(vecs, shifted) + products(vecs, moved))
    sums = contract(vecs, False)
    *sums, grams = sum_group(1, sums + [grams], False)
    back(1, sums)
    lower = factor(grams * (1.0 / PAIRS))
    inverse = lower[:, NV:2 * NV]
    hats = [apply(lower, value, NV) for value in sums]
    scaled = [w * hat for w, hat in zip(weights, hats)]
    part[1, ROWS] = columns(products(scaled, hats) + products(scaled, [xhat[k] for k in range(4)]))
    send_tiles(1, ROWS, TILES)
    middle = small(small(inverse, grams[:, NV:2 * NV]), inverse)
    across = apply(lower, grams[:, 2 * NV:3 * NV], NV)
    coef_ref[1] = jnp.where(lane >= row, lower, 0.0)[:, :NV]
    for i in range(ROWS):
        q2[i] = apply(lower, r1[i], NV)
    spread(1, lower, wide(jnp.concatenate([middle, across], axis=1)))
    proj = ag[1, ROWS]
    coef_ref[2] = proj[:, :NV]
    for i in range(ROWS):
        r1[i] = ag[1, i] + delta(i) * q2[i] - apply(proj, q2[i]) - apply(proj, q1[i], NV)

    vecs = [r1[i] for i in range(ROWS)]
    gm[spot] = columns(products(vecs, vecs))

    def body(d, carry):
        other = lax.rem(spot + d, OCC_WAYS * VIR_WAYS)
        pltpu.make_async_remote_copy(
            src_ref=gm.at[spot], dst_ref=gm.at[spot], send_sem=g_send, recv_sem=g_recv,
            device_id={"occ": other // VIR_WAYS, "vir": lax.rem(other, VIR_WAYS)}, device_id_type=MESH,
        ).start()
        return carry

    lax.fori_loop(1, OCC_WAYS * VIR_WAYS, body, 0)
    wait_bytes(gm.at[pl.ds(0, OCC_WAYS * VIR_WAYS - 1)], g_recv)
    sums = [gm[j] for j in range(OCC_WAYS * VIR_WAYS)]
    while len(sums) > 1:
        sums = [a + b for a, b in zip(sums[0::2], sums[1::2])]
    lower = factor(sums[0] * (1.0 / PAIRS))
    coef_ref[3] = jnp.where(lane >= row, lower, 0.0)[:, :NV]
    for i in range(ROWS):
        next_ref[i] = apply(lower, r1[i], NV)

    for step in range(2):
        wait_bytes(cvir.at[step, pl.ds(0, VIR_WAYS - 1)], cv_send.at[step])
        wait_bytes(cocc.at[step, pl.ds(0, OCC_WAYS - 1)], co_send.at[step])

        @pl.when(owner)
        def _():
            wait_bytes(part.at[step, pl.ds(0, TILES - 1)], rs_send.at[step])
            wait_bytes(rs.at[step, pl.ds(0, AUX_WAYS - 1)], ag_send.at[step])

        @pl.when(jnp.logical_not(owner))
        def _():
            wait_bytes(part.at[step], rs_send.at[step])

    wait_bytes(gm.at[pl.ds(0, OCC_WAYS * VIR_WAYS - 1)], g_send)


def on_device(start_block, factors, eps_occ, eps_vir):
    tile_shape = (NV, LANES)
    dma = pltpu.SemaphoreType.DMA
    anywhere = pl.BlockSpec(memory_space=pltpu.MemorySpace.HBM)
    vmem = pl.BlockSpec(memory_space=pltpu.MemorySpace.VMEM)
    coefs, block = pl.pallas_call(
        kernel,
        out_shape=(
            jax.ShapeDtypeStruct((4, NV, NV), f32),
            jax.ShapeDtypeStruct((ROWS, NV, LANES), f32),
        ),
        in_specs=[anywhere] * 4,
        out_specs=(vmem, vmem),
        scratch_shapes=[
            pltpu.VMEM((ROWS,) + tile_shape, f32),
            pltpu.VMEM((2, ROWS, DEPTH, LANES), bf16),
            pltpu.SMEM((ROWS,), f32),
            pltpu.VMEM((1, LANES), f32),
            pltpu.VMEM((ROWS,) + tile_shape, f32),
            pltpu.VMEM((ROWS,) + tile_shape, f32),
            pltpu.VMEM((ROWS,) + tile_shape, f32),
            pltpu.VMEM((4,) + tile_shape, f32),
            pltpu.VMEM((2, VIR_WAYS, 5) + tile_shape, f32),
            pltpu.VMEM((2, OCC_WAYS, 5) + tile_shape, f32),
            pltpu.VMEM((2, TILES) + tile_shape, f32),
            pltpu.VMEM((2, AUX_WAYS) + tile_shape, f32),
            pltpu.VMEM((2, TILES) + tile_shape, f32),
            pltpu.VMEM((2,) + tile_shape, f32),
            pltpu.VMEM((OCC_WAYS * VIR_WAYS,) + tile_shape, f32),
            dma((3,)), dma((ROWS // GROUP,)),
            dma((2,)), dma((2,)), dma((2,)), dma((2,)),
            dma((2,)), dma((2,)), dma((2,)), dma((2,)),
            dma, dma,
        ],
        compiler_params=pltpu.CompilerParams(
            collective_id=0, has_side_effects=True, vmem_limit_bytes=60 * 1024 * 1024
        ),
        cost_estimate=pl.CostEstimate(flops=200_000_000, bytes_accessed=3_000_000, transcendentals=0),
    )(
        start_block.transpose(1, 0, 2),
        factors.transpose(0, 2, 1, 3),
        eps_occ,
        eps_vir.reshape(1, LANES),
    )
    return coefs, block.transpose(1, 0, 2)


def solution(mesh):
    placed = (P(None, "occ", "vir"), P(None, "aux", "occ", "vir"), P("occ"), P("vir"))
    return jax.shard_map(
        on_device,
        mesh=mesh,
        in_specs=placed,
        out_specs=(P(), P(None, "occ", "vir")),
        check_vma=False,
    )
```

```python
import jax
import jax.numpy as jnp
from jax import lax
from jax.experimental import pallas as pl
from jax.experimental.pallas import tpu as pltpu
from jax.sharding import PartitionSpec as P

AUX_WAYS, OCC_WAYS, VIR_WAYS = 32, 4, 4
NV, ROWS, LANES, DEPTH = 8, 20, 128, 256
PAIRS = 40960
TILES = ROWS + 1
STRIDE, UNSTRIDE = 3, 11
GROUP = 4
MESH = pl.DeviceIdType.MESH
f32, bf16 = jnp.float32, jnp.bfloat16


def split(value):
    high = value.astype(bf16)
    low = (value - high.astype(f32)).astype(bf16)
    return jnp.concatenate([high, low], axis=0)


def merge(value):
    return value[:NV] + value[NV:]


def apply(matrix, value, first=0):
    total = matrix[:, first:first + 1] * value[0:1, :]
    for m in range(1, NV):
        total = total + matrix[:, first + m:first + m + 1] * value[m:m + 1, :]
    return total


def iotas():
    return (
        lax.broadcasted_iota(jnp.int32, (NV, LANES), 0),
        lax.broadcasted_iota(jnp.int32, (NV, LANES), 1),
    )


def factor(gram):
    row, lane = iotas()
    work = jnp.where(lane < NV, gram, jnp.where(lane == row + NV, 1.0, 0.0))
    scale = jnp.ones((NV, 1), f32)
    rows1 = lax.broadcasted_iota(jnp.int32, (NV, 1), 0)
    for k in range(NV):
        pivot = work[k:k + 1, k:k + 1]
        scale = jnp.where(rows1 == k, pivot, scale)
        if k < NV - 1:
            ratio = jnp.where(rows1 > k, work[:, k:k + 1] / pivot, 0.0)
            work = work - ratio * work[k:k + 1, :]
    return work * (1.0 / jnp.sqrt(scale))


def columns(sums):
    _, lane = iotas()
    out = jnp.zeros((NV, LANES), f32)
    for m, value in enumerate(sums):
        out = jnp.where(lane == m, jnp.sum(value, axis=1, keepdims=True), out)
    return out


def products(lefts, rights):
    sums = []
    for m in range(NV):
        total = lefts[0] * rights[0][m:m + 1, :]
        for left, right in zip(lefts[1:], rights[1:]):
            total = total + left * right[m:m + 1, :]
        sums.append(total)
    return sums


def kernel(
    start_hbm, fac_hbm, occ_hbm, vir_hbm,
    coef_ref, resid_ref,
    start, fac, eocc, evir, q1, q2, r1, xhat,
    cvir, cocc, part, rs, ag, mine, gm,
    in_sem, fac_sem, cv_send, cv_recv, co_send, co_recv,
    rs_send, rs_recv, ag_send, ag_recv, g_send, g_recv,
):
    aux = lax.axis_index("aux")
    occ = lax.axis_index("occ")
    vir = lax.axis_index("vir")
    spot = occ * VIR_WAYS + vir
    core = lax.rem(vir, 2)

    def tile_of(device):
        return lax.rem((device + core) * UNSTRIDE, AUX_WAYS)

    tile = tile_of(aux)
    owner = tile < TILES

    loads = [
        pltpu.make_async_copy(start_hbm, start, in_sem.at[0]),
        pltpu.make_async_copy(occ_hbm, eocc, in_sem.at[1]),
        pltpu.make_async_copy(vir_hbm, evir, in_sem.at[2]),
    ]
    fac_loads = [
        pltpu.make_async_copy(
            fac_hbm.at[:, pl.ds(GROUP * c, GROUP)], fac.at[:, pl.ds(GROUP * c, GROUP)], fac_sem.at[c]
        )
        for c in range(ROWS // GROUP)
    ]
    for load in loads + fac_loads:
        load.start()

    barrier = pltpu.get_barrier_semaphore()

    def greet_aux(d, carry):
        pl.semaphore_signal(
            barrier, inc=1, device_id={"aux": lax.rem(aux + d, AUX_WAYS)}, device_id_type=MESH
        )
        return carry

    def greet_spot(d, carry):
        other = lax.rem(spot + d, OCC_WAYS * VIR_WAYS)
        pl.semaphore_signal(
            barrier, inc=1,
            device_id={"occ": other // VIR_WAYS, "vir": lax.rem(other, VIR_WAYS)}, device_id_type=MESH,
        )
        return carry

    lax.fori_loop(1, AUX_WAYS, greet_aux, 0)
    lax.fori_loop(1, OCC_WAYS * VIR_WAYS, greet_spot, 0)

    for load in loads:
        load.wait()

    def delta(i):
        return evir[...] - eocc[i]

    def contract(source, waits):
        sums = [None, None]
        for i in range(0, ROWS, 2):
            if waits and i % GROUP == 0:
                fac_loads[i // GROUP].wait()
            left = jnp.concatenate([split(source[i]), split(source[i + 1])], axis=1)
            for s in range(2):
                right = jnp.concatenate([fac[s, i], fac[s, i + 1]], axis=1)
                term = lax.dot_general(
                    left, right, (((1,), (1,)), ((), ())), preferred_element_type=f32
                )
                sums[s] = term if sums[s] is None else sums[s] + term
        return [merge(sums[s])[:, LANES * h:LANES * (h + 1)] for s in range(2) for h in range(2)]

    def wait_bytes(ref, sem):
        pltpu.make_async_copy(ref, ref, sem).wait()

    def sum_group(step, tiles, first):
        count = len(tiles)
        for index, value in enumerate(tiles):
            cvir[step, vir, index] = value
        if first:
            pl.semaphore_wait(barrier, AUX_WAYS - 1 + OCC_WAYS * VIR_WAYS - 1)
        for d in range(1, VIR_WAYS):
            pltpu.make_async_remote_copy(
                src_ref=cvir.at[step, vir], dst_ref=cvir.at[step, vir],
                send_sem=cv_send.at[step], recv_sem=cv_recv.at[step],
                device_id={"vir": lax.rem(vir + d, VIR_WAYS)}, device_id_type=MESH,
            ).start()
        wait_bytes(cvir.at[step, pl.ds(0, VIR_WAYS - 1)], cv_recv.at[step])
        for index in range(count):
            cocc[step, occ, index] = (
                (cvir[step, 0, index] + cvir[step, 1, index])
                + (cvir[step, 2, index] + cvir[step, 3, index])
            )
        for d in range(1, OCC_WAYS):
            pltpu.make_async_remote_copy(
                src_ref=cocc.at[step, occ], dst_ref=cocc.at[step, occ],
                send_sem=co_send.at[step], recv_sem=co_recv.at[step],
                device_id={"occ": lax.rem(occ + d, OCC_WAYS)}, device_id_type=MESH,
            ).start()
        wait_bytes(cocc.at[step, pl.ds(0, OCC_WAYS - 1)], co_recv.at[step])
        return [
            (cocc[step, 0, index] + cocc[step, 1, index])
            + (cocc[step, 2, index] + cocc[step, 3, index])
            for index in range(count)
        ]

    def both_ways(action):
        def body(d, carry):
            action(d)
            action(AUX_WAYS - d)
            return carry

        lax.fori_loop(1, AUX_WAYS // 2, body, 0)
        action(AUX_WAYS // 2)

    def send_tile(step, t, target):
        pltpu.make_async_remote_copy(
            src_ref=part.at[step, t], dst_ref=rs.at[step, aux],
            send_sem=rs_send.at[step], recv_sem=rs_recv.at[step],
            device_id={"aux": target}, device_id_type=MESH,
        ).start()

    def send_rows(step):
        def action(d):
            target = lax.rem(aux + d, AUX_WAYS)
            t = tile_of(target)

            @pl.when(t < ROWS)
            def _():
                send_tile(step, t, target)

        both_ways(action)

        @pl.when(tile < ROWS)
        def _():
            rs[step, aux] = part[step, tile]

    def send_small(step):
        target = lax.rem(ROWS * STRIDE - core, AUX_WAYS)

        @pl.when(target != aux)
        def _():
            send_tile(step, ROWS, target)

        @pl.when(target == aux)
        def _():
            rs[step, aux] = part[step, ROWS]

    def back(step, sums):
        scaled = [
            split(jnp.concatenate([2.0 * sums[0], 2.0 * sums[1]], axis=1)),
            split(jnp.concatenate([-sums[2], -sums[3]], axis=1)),
        ]
        for i in range(0, ROWS, 2):
            both = None
            for s in range(2):
                right = jnp.concatenate([fac[s, i], fac[s, i + 1]], axis=1)
                term = lax.dot_general(
                    scaled[s], right, (((1,), (0,)), ((), ())), preferred_element_type=f32
                )
                both = term if both is None else both + term
            both = merge(both)
            part[step, i] = both[:, :LANES]
            part[step, i + 1] = both[:, LANES:]
        send_rows(step)

    def spread(step, lower, extra):
        @pl.when(owner)
        def _():
            wait_bytes(rs.at[step, pl.ds(0, AUX_WAYS - 1)], rs_recv.at[step])
            sums = [rs[step, j] for j in range(AUX_WAYS)]
            while len(sums) > 1:
                sums = [a + b for a, b in zip(sums[0::2], sums[1::2])]

            @pl.when(tile < ROWS)
            def _():
                mine[step] = apply(lower, sums[0], NV)

            @pl.when(tile == ROWS)
            def _():
                mine[step] = (sums[0] + extra) * (1.0 / PAIRS)

            def action(d):
                pltpu.make_async_remote_copy(
                    src_ref=mine.at[step], dst_ref=ag.at[step, tile],
                    send_sem=ag_send.at[step], recv_sem=ag_recv.at[step],
                    device_id={"aux": lax.rem(aux + d, AUX_WAYS)}, device_id_type=MESH,
                ).start()

            both_ways(action)
            ag[step, tile] = mine[step]
            wait_bytes(ag.at[step, pl.ds(0, TILES - 1)], ag_recv.at[step])

        @pl.when(jnp.logical_not(owner))
        def _():
            wait_bytes(ag.at[step], ag_recv.at[step])

    def small(left, right):
        return lax.dot_general(
            left, right, (((1,), (1,)), ((), ())),
            precision=lax.Precision.HIGHEST, preferred_element_type=f32,
        )

    def wide(value):
        return jnp.concatenate(
            [value, jnp.zeros((value.shape[0], LANES - value.shape[1]), f32)], axis=1
        )

    row, lane = iotas()
    weights = [2.0, 2.0, -1.0, -1.0]

    vecs = [start[i] for i in range(ROWS)]
    shifted = [vecs[i] * delta(i) for i in range(ROWS)]
    grams = columns(products(vecs, vecs) + products(vecs, shifted))
    sums = contract(vecs, True)
    *sums, grams = sum_group(0, sums + [grams], True)
    back(0, sums)
    lower = factor(grams * (1.0 / PAIRS))
    inverse = lower[:, NV:2 * NV]
    hats = [apply(lower, value, NV) for value in sums]
    for index in range(4):
        xhat[index] = hats[index]
    part[0, ROWS] = columns(products([w * hat for w, hat in zip(weights, hats)], hats))
    send_small(0)
    middle = small(small(inverse, grams[:, NV:2 * NV]), inverse)
    for i in range(ROWS):
        q1[i] = apply(lower, start[i], NV)
    spread(0, lower, wide(middle))
    proj = ag[0, ROWS]
    coef_ref[0] = proj
    for i in range(ROWS):
        r1[i] = ag[0, i] + delta(i) * q1[i] - apply(proj, q1[i])

    vecs = [r1[i] for i in range(ROWS)]
    moved = [delta(i) * q1[i] for i in range(ROWS)]
    shifted = [vecs[i] * delta(i) for i in range(ROWS)]
    grams = columns(products(vecs, vecs) + products(vecs, shifted) + products(vecs, moved))
    sums = contract(vecs, False)
    *sums, grams = sum_group(1, sums + [grams], False)
    back(1, sums)
    lower = factor(grams * (1.0 / PAIRS))
    inverse = lower[:, NV:2 * NV]
    hats = [apply(lower, value, NV) for value in sums]
    scaled = [w * hat for w, hat in zip(weights, hats)]
    part[1, ROWS] = columns(products(scaled, hats) + products(scaled, [xhat[k] for k in range(4)]))
    send_small(1)
    middle = small(small(inverse, grams[:, NV:2 * NV]), inverse)
    across = apply(lower, grams[:, 2 * NV:3 * NV], NV)
    coef_ref[1] = jnp.where(lane >= row, lower, 0.0)
    for i in range(ROWS):
        q2[i] = apply(lower, r1[i], NV)
    spread(1, lower, wide(jnp.concatenate([middle, across], axis=1)))
    proj = ag[1, ROWS]
    coef_ref[2] = proj
    for i in range(ROWS):
        resid_ref[i] = ag[1, i] + delta(i) * q2[i] - apply(proj, q2[i]) - apply(proj, q1[i], NV)

    vecs = [resid_ref[i] for i in range(ROWS)]
    gm[spot] = columns(products(vecs, vecs))

    def body(d, carry):
        other = lax.rem(spot + d, OCC_WAYS * VIR_WAYS)
        pltpu.make_async_remote_copy(
            src_ref=gm.at[spot], dst_ref=gm.at[spot], send_sem=g_send, recv_sem=g_recv,
            device_id={"occ": other // VIR_WAYS, "vir": lax.rem(other, VIR_WAYS)}, device_id_type=MESH,
        ).start()
        return carry

    lax.fori_loop(1, OCC_WAYS * VIR_WAYS, body, 0)
    wait_bytes(gm.at[pl.ds(0, OCC_WAYS * VIR_WAYS - 1)], g_recv)
    sums = [gm[j] for j in range(OCC_WAYS * VIR_WAYS)]
    while len(sums) > 1:
        sums = [a + b for a, b in zip(sums[0::2], sums[1::2])]
    coef_ref[3] = sums[0] * (1.0 / PAIRS)

    for step in range(2):
        wait_bytes(cvir.at[step, pl.ds(0, VIR_WAYS - 1)], cv_send.at[step])
        wait_bytes(cocc.at[step, pl.ds(0, OCC_WAYS - 1)], co_send.at[step])

        @pl.when(owner)
        def _():
            wait_bytes(part.at[step, pl.ds(0, TILES - 1)], rs_send.at[step])
            wait_bytes(rs.at[step, pl.ds(0, AUX_WAYS - 1)], ag_send.at[step])

        @pl.when(jnp.logical_not(owner))
        def _():
            wait_bytes(part.at[step], rs_send.at[step])

    wait_bytes(gm.at[pl.ds(0, OCC_WAYS * VIR_WAYS - 1)], g_send)


def finish(small_ref, resid_ref, coef_ref, next_ref):
    row, lane = iotas()
    lower = factor(small_ref[3])
    for k in range(3):
        coef_ref[k] = small_ref[k][:, :NV]
    coef_ref[3] = jnp.where(lane >= row, lower, 0.0)[:, :NV]
    for i in range(ROWS):
        next_ref[i] = apply(lower, resid_ref[i], NV)


def on_device(start_block, factors, eps_occ, eps_vir):
    tile_shape = (NV, LANES)
    dma = pltpu.SemaphoreType.DMA
    anywhere = pl.BlockSpec(memory_space=pltpu.MemorySpace.HBM)
    vmem = pl.BlockSpec(memory_space=pltpu.MemorySpace.VMEM)
    small, resid = pl.pallas_call(
        kernel,
        out_shape=(
            pltpu.VMEM((4,) + tile_shape, f32),
            pltpu.VMEM((ROWS,) + tile_shape, f32),
        ),
        in_specs=[anywhere] * 4,
        out_specs=(vmem, vmem),
        scratch_shapes=[
            pltpu.VMEM((ROWS,) + tile_shape, f32),
            pltpu.VMEM((2, ROWS, DEPTH, LANES), bf16),
            pltpu.SMEM((ROWS,), f32),
            pltpu.VMEM((1, LANES), f32),
            pltpu.VMEM((ROWS,) + tile_shape, f32),
            pltpu.VMEM((ROWS,) + tile_shape, f32),
            pltpu.VMEM((ROWS,) + tile_shape, f32),
            pltpu.VMEM((4,) + tile_shape, f32),
            pltpu.VMEM((2, VIR_WAYS, 5) + tile_shape, f32),
            pltpu.VMEM((2, OCC_WAYS, 5) + tile_shape, f32),
            pltpu.VMEM((2, TILES) + tile_shape, f32),
            pltpu.VMEM((2, AUX_WAYS) + tile_shape, f32),
            pltpu.VMEM((2, TILES) + tile_shape, f32),
            pltpu.VMEM((2,) + tile_shape, f32),
            pltpu.VMEM((OCC_WAYS * VIR_WAYS,) + tile_shape, f32),
            dma((3,)), dma((ROWS // GROUP,)),
            dma((2,)), dma((2,)), dma((2,)), dma((2,)),
            dma((2,)), dma((2,)), dma((2,)), dma((2,)),
            dma, dma,
        ],
        compiler_params=pltpu.CompilerParams(
            collective_id=0, has_side_effects=True, vmem_limit_bytes=60 * 1024 * 1024
        ),
        cost_estimate=pl.CostEstimate(flops=200_000_000, bytes_accessed=3_000_000, transcendentals=0),
    )(
        start_block.transpose(1, 0, 2),
        factors.transpose(0, 2, 1, 3),
        eps_occ,
        eps_vir.reshape(1, LANES),
    )
    coefs, block = pl.pallas_call(
        finish,
        out_shape=(
            jax.ShapeDtypeStruct((4, NV, NV), f32),
            jax.ShapeDtypeStruct((ROWS,) + tile_shape, f32),
        ),
        in_specs=[vmem] * 2,
        out_specs=(vmem, vmem),
        cost_estimate=pl.CostEstimate(flops=400_000, bytes_accessed=200_000, transcendentals=0),
    )(small, resid)
    return coefs, block.transpose(1, 0, 2)


def solution(mesh):
    placed = (P(None, "occ", "vir"), P(None, "aux", "occ", "vir"), P("occ"), P("vir"))
    return jax.shard_map(
        on_device,
        mesh=mesh,
        in_specs=placed,
        out_specs=(P(), P(None, "occ", "vir")),
        check_vma=False,
    )
```

```python
import jax
import jax.numpy as jnp
from jax import lax
from jax.experimental import pallas as pl
from jax.experimental.pallas import tpu as pltpu
from jax.sharding import PartitionSpec as P

OCC_WAYS, VIR_WAYS = 4, 4
NV, ROWS, LANES, DEPTH = 8, 20, 128, 256
PAIRS = 40960
TILES = ROWS + 1
NEAR, BLOCKS, Z, SHARE = 8, 4, 16, 3
OWNERS = TILES // SHARE
GROUP = 4
MESH = pl.DeviceIdType.MESH
f32, bf16 = jnp.float32, jnp.bfloat16


def split(value):
    high = value.astype(bf16)
    low = (value - high.astype(f32)).astype(bf16)
    return jnp.concatenate([high, low], axis=0)


def merge(value):
    return value[:NV] + value[NV:]


def apply(matrix, value, first=0):
    total = matrix[:, first:first + 1] * value[0:1, :]
    for m in range(1, NV):
        total = total + matrix[:, first + m:first + m + 1] * value[m:m + 1, :]
    return total


def iotas():
    return (
        lax.broadcasted_iota(jnp.int32, (NV, LANES), 0),
        lax.broadcasted_iota(jnp.int32, (NV, LANES), 1),
    )


def factor(gram):
    row, lane = iotas()
    work = jnp.where(lane < NV, gram, jnp.where(lane == row + NV, 1.0, 0.0))
    scale = jnp.ones((NV, 1), f32)
    rows1 = lax.broadcasted_iota(jnp.int32, (NV, 1), 0)
    for k in range(NV):
        pivot = work[k:k + 1, k:k + 1]
        scale = jnp.where(rows1 == k, pivot, scale)
        if k < NV - 1:
            ratio = jnp.where(rows1 > k, work[:, k:k + 1] / pivot, 0.0)
            work = work - ratio * work[k:k + 1, :]
    return work * (1.0 / jnp.sqrt(scale))


def columns(sums):
    _, lane = iotas()
    out = jnp.zeros((NV, LANES), f32)
    for m, value in enumerate(sums):
        out = jnp.where(lane == m, jnp.sum(value, axis=1, keepdims=True), out)
    return out


def products(lefts, rights):
    sums = []
    for m in range(NV):
        total = lefts[0] * rights[0][m:m + 1, :]
        for left, right in zip(lefts[1:], rights[1:]):
            total = total + left * right[m:m + 1, :]
        sums.append(total)
    return sums


def kernel(
    start_hbm, fac_hbm, occ_hbm, vir_hbm,
    coef_ref, resid_ref,
    start, fac, eocc, evir, q1, q2, r1, xhat,
    cvir, cocc, part, rs, cx, ag, gm,
    in_sem, fac_sem, cv_send, cv_recv, co_send, co_recv,
    rs_send, rs_recv, cx_send, cx_recv, ag_send, ag_recv, g_send, g_recv,
):
    aux = lax.axis_index("aux")
    occ = lax.axis_index("occ")
    vir = lax.axis_index("vir")
    spot = occ * VIR_WAYS + vir
    core = lax.rem(vir, 2)
    side = aux // Z
    block = lax.rem(aux, Z) // BLOCKS
    place = lax.rem(aux, BLOCKS)
    role = lax.rem(side * BLOCKS + place + BLOCKS * core, NEAR)
    owner = role < OWNERS
    own = pl.ds(role * SHARE, SHARE)

    def near(other):
        spot_of = lax.rem(other + BLOCKS * core, NEAR)
        return {"aux": (spot_of // BLOCKS) * Z + block * BLOCKS + lax.rem(spot_of, BLOCKS)}

    def far(d):
        return {"aux": side * Z + lax.rem(block + d, BLOCKS) * BLOCKS + place}

    def mate(d):
        other = lax.rem(spot + d, OCC_WAYS * VIR_WAYS)
        return {"occ": other // VIR_WAYS, "vir": lax.rem(other, VIR_WAYS)}

    peers = [near(lax.rem(role + d, NEAR)) for d in range(1, NEAR)]
    crosses = [far(d) for d in range(1, BLOCKS)]
    mates = [mate(d) for d in range(1, OCC_WAYS * VIR_WAYS)]

    loads = [
        pltpu.make_async_copy(start_hbm, start, in_sem.at[0]),
        pltpu.make_async_copy(occ_hbm, eocc, in_sem.at[1]),
        pltpu.make_async_copy(vir_hbm, evir, in_sem.at[2]),
    ]
    fac_loads = [
        pltpu.make_async_copy(
            fac_hbm.at[:, pl.ds(GROUP * c, GROUP)], fac.at[:, pl.ds(GROUP * c, GROUP)], fac_sem.at[c]
        )
        for c in range(ROWS // GROUP)
    ]
    for load in loads + fac_loads:
        load.start()

    barrier = pltpu.get_barrier_semaphore()

    greeted = mates + peers + crosses
    for device in greeted:
        pl.semaphore_signal(barrier, inc=1, device_id=device, device_id_type=MESH)

    for load in loads:
        load.wait()

    def delta(i):
        return evir[...] - eocc[i]

    def contract(source, waits):
        sums = [None, None]
        for i in range(0, ROWS, 2):
            if waits and i % GROUP == 0:
                fac_loads[i // GROUP].wait()
            left = jnp.concatenate([split(source[i]), split(source[i + 1])], axis=1)
            for s in range(2):
                right = jnp.concatenate([fac[s, i], fac[s, i + 1]], axis=1)
                term = lax.dot_general(
                    left, right, (((1,), (1,)), ((), ())), preferred_element_type=f32
                )
                sums[s] = term if sums[s] is None else sums[s] + term
        return [merge(sums[s])[:, LANES * h:LANES * (h + 1)] for s in range(2) for h in range(2)]

    def wait_bytes(ref, sem):
        pltpu.make_async_copy(ref, ref, sem).wait()

    def sum_group(step, tiles, first):
        count = len(tiles)
        for index, value in enumerate(tiles):
            cvir[step, vir, index] = value
        if first:
            pl.semaphore_wait(barrier, len(greeted))
        for d in range(1, VIR_WAYS):
            pltpu.make_async_remote_copy(
                src_ref=cvir.at[step, vir], dst_ref=cvir.at[step, vir],
                send_sem=cv_send.at[step], recv_sem=cv_recv.at[step],
                device_id={"vir": lax.rem(vir + d, VIR_WAYS)}, device_id_type=MESH,
            ).start()
        wait_bytes(cvir.at[step, pl.ds(0, VIR_WAYS - 1)], cv_recv.at[step])
        for index in range(count):
            cocc[step, occ, index] = (
                (cvir[step, 0, index] + cvir[step, 1, index])
                + (cvir[step, 2, index] + cvir[step, 3, index])
            )
        for d in range(1, OCC_WAYS):
            pltpu.make_async_remote_copy(
                src_ref=cocc.at[step, occ], dst_ref=cocc.at[step, occ],
                send_sem=co_send.at[step], recv_sem=co_recv.at[step],
                device_id={"occ": lax.rem(occ + d, OCC_WAYS)}, device_id_type=MESH,
            ).start()
        wait_bytes(cocc.at[step, pl.ds(0, OCC_WAYS - 1)], co_recv.at[step])
        return [
            (cocc[step, 0, index] + cocc[step, 1, index])
            + (cocc[step, 2, index] + cocc[step, 3, index])
            for index in range(count)
        ]

    def send(source, target, sems, device):
        pltpu.make_async_remote_copy(
            src_ref=source, dst_ref=target, send_sem=sems[0], recv_sem=sems[1],
            device_id=device, device_id_type=MESH,
        ).start()

    def scatter(step):
        for d in range(1, NEAR):
            other = lax.rem(role + d, NEAR)

            @pl.when(other < OWNERS)
            def _():
                send(
                    part.at[step, pl.ds(other * SHARE, SHARE)], rs.at[step, role],
                    (rs_send.at[step], rs_recv.at[step]), peers[d - 1],
                )

        @pl.when(owner)
        def _():
            rs[step, role] = part[step, own]

    def back(step, sums):
        scaled = [
            split(jnp.concatenate([2.0 * sums[0], 2.0 * sums[1]], axis=1)),
            split(jnp.concatenate([-sums[2], -sums[3]], axis=1)),
        ]
        for i in range(0, ROWS, 2):
            both = None
            for s in range(2):
                right = jnp.concatenate([fac[s, i], fac[s, i + 1]], axis=1)
                term = lax.dot_general(
                    scaled[s], right, (((1,), (0,)), ((), ())), preferred_element_type=f32
                )
                both = term if both is None else both + term
            both = merge(both)
            part[step, i] = both[:, :LANES]
            part[step, i + 1] = both[:, LANES:]
        scatter(step)

    def spread(step, lower, turned, extra):
        @pl.when(owner)
        def _():
            wait_bytes(rs.at[step, pl.ds(0, NEAR - 1)], rs_recv.at[step])
            sums = [rs[step, j] for j in range(NEAR)]
            while len(sums) > 1:
                sums = [a + b for a, b in zip(sums[0::2], sums[1::2])]
            cx[step, block] = sums[0]
            for d in range(1, BLOCKS):
                send(
                    cx.at[step, block], cx.at[step, block],
                    (cx_send.at[step], cx_recv.at[step]), crosses[d - 1],
                )
            wait_bytes(cx.at[step, pl.ds(0, BLOCKS - 1)], cx_recv.at[step])
            total = (cx[step, 0] + cx[step, 1]) + (cx[step, 2] + cx[step, 3])
            for k in range(SHARE - 1):
                ag[step, role * SHARE + k] = apply(lower, total[k], NV)
            last = role * SHARE + SHARE - 1

            @pl.when(role < OWNERS - 1)
            def _():
                ag[step, last] = apply(lower, total[SHARE - 1], NV)

            @pl.when(role == OWNERS - 1)
            def _():
                half = apply(lower, (total[SHARE - 1] + extra) * (1.0 / PAIRS), NV)
                whole = apply(half, turned)
                ag[step, last] = jnp.where(lane < NV, whole, half)

            for device in peers:
                send(
                    ag.at[step, own], ag.at[step, own],
                    (ag_send.at[step], ag_recv.at[step]), device,
                )
            wait_bytes(ag.at[step, pl.ds(0, TILES - SHARE)], ag_recv.at[step])

        @pl.when(jnp.logical_not(owner))
        def _():
            wait_bytes(ag.at[step], ag_recv.at[step])

    def small(left, right):
        return lax.dot_general(
            left, right, (((1,), (1,)), ((), ())),
            precision=lax.Precision.HIGHEST, preferred_element_type=f32,
        )

    def wide(value):
        return jnp.concatenate(
            [value, jnp.zeros((value.shape[0], LANES - value.shape[1]), f32)], axis=1
        )

    row, lane = iotas()
    weights = [2.0, 2.0, -1.0, -1.0]

    def turn(lower):
        return wide(small(jnp.where(lane == row, 1.0, 0.0)[:, :NV], lower[:, NV:2 * NV]))

    vecs = [start[i] for i in range(ROWS)]
    shifted = [vecs[i] * delta(i) for i in range(ROWS)]
    grams = columns(products(vecs, vecs) + products(vecs, shifted))
    sums = contract(vecs, True)
    *sums, grams = sum_group(0, sums + [grams], True)
    part[0, ROWS] = columns(products([w * v for w, v in zip(weights, sums)], sums))
    back(0, sums)
    lower = factor(grams * (1.0 / PAIRS))
    for index in range(4):
        xhat[index] = apply(lower, sums[index], NV)
    for i in range(ROWS):
        q1[i] = apply(lower, start[i], NV)
    extra = jnp.where(lane < NV, pltpu.roll(grams, LANES - NV, 1), 0.0)
    spread(0, lower, turn(lower), extra)
    proj = ag[0, ROWS]
    coef_ref[0] = proj
    for i in range(ROWS):
        r1[i] = ag[0, i] + delta(i) * q1[i] - apply(proj, q1[i])

    vecs = [r1[i] for i in range(ROWS)]
    moved = [delta(i) * q1[i] for i in range(ROWS)]
    shifted = [vecs[i] * delta(i) for i in range(ROWS)]
    grams = columns(products(vecs, vecs) + products(vecs, shifted) + products(vecs, moved))
    sums = contract(vecs, False)
    *sums, grams = sum_group(1, sums + [grams], False)
    scaled = [w * v for w, v in zip(weights, sums)]
    part[1, ROWS] = columns(products(scaled, sums) + products(scaled, [xhat[k] for k in range(4)]))
    back(1, sums)
    lower = factor(grams * (1.0 / PAIRS))
    coef_ref[1] = jnp.where(lane >= row, lower, 0.0)
    for i in range(ROWS):
        q2[i] = apply(lower, r1[i], NV)
    extra = jnp.where(lane < 2 * NV, pltpu.roll(grams, LANES - NV, 1), 0.0)
    spread(1, lower, turn(lower), extra)
    proj = ag[1, ROWS]
    coef_ref[2] = proj
    for i in range(ROWS):
        resid_ref[i] = ag[1, i] + delta(i) * q2[i] - apply(proj, q2[i]) - apply(proj, q1[i], NV)

    vecs = [resid_ref[i] for i in range(ROWS)]
    gm[spot] = columns(products(vecs, vecs))

    for device in mates:
        send(gm.at[spot], gm.at[spot], (g_send, g_recv), device)
    wait_bytes(gm.at[pl.ds(0, OCC_WAYS * VIR_WAYS - 1)], g_recv)
    sums = [gm[j] for j in range(OCC_WAYS * VIR_WAYS)]
    while len(sums) > 1:
        sums = [a + b for a, b in zip(sums[0::2], sums[1::2])]
    coef_ref[3] = sums[0] * (1.0 / PAIRS)

    for step in range(2):
        wait_bytes(cvir.at[step, pl.ds(0, VIR_WAYS - 1)], cv_send.at[step])
        wait_bytes(cocc.at[step, pl.ds(0, OCC_WAYS - 1)], co_send.at[step])

        @pl.when(owner)
        def _():
            wait_bytes(part.at[step, pl.ds(0, TILES - SHARE)], rs_send.at[step])
            wait_bytes(cx.at[step, pl.ds(0, BLOCKS - 1)], cx_send.at[step])
            wait_bytes(rs.at[step, pl.ds(0, NEAR - 1)], ag_send.at[step])

        @pl.when(jnp.logical_not(owner))
        def _():
            wait_bytes(part.at[step], rs_send.at[step])

    wait_bytes(gm.at[pl.ds(0, OCC_WAYS * VIR_WAYS - 1)], g_send)


def finish(small_ref, resid_ref, coef_ref, next_ref):
    row, lane = iotas()
    lower = factor(small_ref[3])
    for k in range(3):
        coef_ref[k] = small_ref[k][:, :NV]
    coef_ref[3] = jnp.where(lane >= row, lower, 0.0)[:, :NV]
    for i in range(ROWS):
        next_ref[i] = apply(lower, resid_ref[i], NV)


def on_device(start_block, factors, eps_occ, eps_vir):
    tile_shape = (NV, LANES)
    dma = pltpu.SemaphoreType.DMA
    anywhere = pl.BlockSpec(memory_space=pltpu.MemorySpace.HBM)
    vmem = pl.BlockSpec(memory_space=pltpu.MemorySpace.VMEM)
    small, resid = pl.pallas_call(
        kernel,
        out_shape=(
            pltpu.VMEM((4,) + tile_shape, f32),
            pltpu.VMEM((ROWS,) + tile_shape, f32),
        ),
        in_specs=[anywhere] * 4,
        out_specs=(vmem, vmem),
        scratch_shapes=[
            pltpu.VMEM((ROWS,) + tile_shape, f32),
            pltpu.VMEM((2, ROWS, DEPTH, LANES), bf16),
            pltpu.SMEM((ROWS,), f32),
            pltpu.VMEM((1, LANES), f32),
            pltpu.VMEM((ROWS,) + tile_shape, f32),
            pltpu.VMEM((ROWS,) + tile_shape, f32),
            pltpu.VMEM((ROWS,) + tile_shape, f32),
            pltpu.VMEM((4,) + tile_shape, f32),
            pltpu.VMEM((2, VIR_WAYS, 5) + tile_shape, f32),
            pltpu.VMEM((2, OCC_WAYS, 5) + tile_shape, f32),
            pltpu.VMEM((2, TILES) + tile_shape, f32),
            pltpu.VMEM((2, NEAR, SHARE) + tile_shape, f32),
            pltpu.VMEM((2, BLOCKS, SHARE) + tile_shape, f32),
            pltpu.VMEM((2, TILES) + tile_shape, f32),
            pltpu.VMEM((OCC_WAYS * VIR_WAYS,) + tile_shape, f32),
            dma((3,)), dma((ROWS // GROUP,)),
            dma((2,)), dma((2,)), dma((2,)), dma((2,)),
            dma((2,)), dma((2,)), dma((2,)), dma((2,)), dma((2,)), dma((2,)),
            dma, dma,
        ],
        compiler_params=pltpu.CompilerParams(
            collective_id=0, has_side_effects=True, vmem_limit_bytes=60 * 1024 * 1024
        ),
        cost_estimate=pl.CostEstimate(flops=200_000_000, bytes_accessed=3_000_000, transcendentals=0),
    )(
        start_block.transpose(1, 0, 2),
        factors.transpose(0, 2, 1, 3),
        eps_occ,
        eps_vir.reshape(1, LANES),
    )
    coefs, block = pl.pallas_call(
        finish,
        out_shape=(
            jax.ShapeDtypeStruct((4, NV, NV), f32),
            jax.ShapeDtypeStruct((ROWS,) + tile_shape, f32),
        ),
        in_specs=[vmem] * 2,
        out_specs=(vmem, vmem),
        compiler_params=pltpu.CompilerParams(vmem_limit_bytes=4 * 1024 * 1024),
        cost_estimate=pl.CostEstimate(flops=400_000, bytes_accessed=200_000, transcendentals=0),
    )(small, resid)
    return coefs, block.transpose(1, 0, 2)


def solution(mesh):
    placed = (P(None, "occ", "vir"), P(None, "aux", "occ", "vir"), P("occ"), P("vir"))
    return jax.shard_map(
        on_device,
        mesh=mesh,
        in_specs=placed,
        out_specs=(P(), P(None, "occ", "vir")),
        check_vma=False,
    )
```

```python
import jax
import jax.numpy as jnp
from jax import lax
from jax.experimental import pallas as pl
from jax.experimental.pallas import tpu as pltpu
from jax.sharding import PartitionSpec as P

OCC_WAYS, VIR_WAYS = 4, 4
NV, ROWS, LANES, DEPTH = 8, 20, 128, 256
PAIRS = 40960
TILES = ROWS + 1
NEAR, BLOCKS, Z, SHARE = 8, 4, 16, 3
OWNERS = TILES // SHARE
GROUP = 4
MESH = pl.DeviceIdType.MESH
f32, bf16 = jnp.float32, jnp.bfloat16


def split(value):
    high = value.astype(bf16)
    low = (value - high.astype(f32)).astype(bf16)
    return jnp.concatenate([high, low], axis=0)


def merge(value):
    return value[:NV] + value[NV:]


def apply(matrix, value, first=0):
    total = matrix[:, first:first + 1] * value[0:1, :]
    for m in range(1, NV):
        total = total + matrix[:, first + m:first + m + 1] * value[m:m + 1, :]
    return total


def iotas():
    return (
        lax.broadcasted_iota(jnp.int32, (NV, LANES), 0),
        lax.broadcasted_iota(jnp.int32, (NV, LANES), 1),
    )


def factor(gram):
    row, lane = iotas()
    work = jnp.where(lane < NV, gram, jnp.where(lane == row + NV, 1.0, 0.0))
    scale = jnp.ones((NV, 1), f32)
    rows1 = lax.broadcasted_iota(jnp.int32, (NV, 1), 0)
    for k in range(NV):
        pivot = work[k:k + 1, k:k + 1]
        scale = jnp.where(rows1 == k, pivot, scale)
        if k < NV - 1:
            ratio = jnp.where(rows1 > k, work[:, k:k + 1] / pivot, 0.0)
            work = work - ratio * work[k:k + 1, :]
    return work * (1.0 / jnp.sqrt(scale))


def columns(sums):
    _, lane = iotas()
    out = jnp.zeros((NV, LANES), f32)
    for m, value in enumerate(sums):
        out = jnp.where(lane == m, jnp.sum(value, axis=1, keepdims=True), out)
    return out


def products(lefts, rights):
    sums = []
    for m in range(NV):
        total = lefts[0] * rights[0][m:m + 1, :]
        for left, right in zip(lefts[1:], rights[1:]):
            total = total + left * right[m:m + 1, :]
        sums.append(total)
    return sums


def kernel(
    start_hbm, fac_hbm, occ_hbm, vir_hbm,
    coef_ref, resid_ref,
    start, fac, eocc, evir, q1, q2, r1, xhat,
    cm, part, rs, cx, ag, gm,
    in_sem, fac_sem, cm_send, cm_recv,
    rs_send, rs_recv, cx_send, cx_recv, ag_send, ag_recv, g_send, g_recv,
):
    aux = lax.axis_index("aux")
    occ = lax.axis_index("occ")
    vir = lax.axis_index("vir")
    spot = occ * VIR_WAYS + vir
    core = lax.rem(vir, 2)
    side = aux // Z
    block = lax.rem(aux, Z) // BLOCKS
    place = lax.rem(aux, BLOCKS)
    role = lax.rem(side * BLOCKS + place + BLOCKS * core, NEAR)
    owner = role < OWNERS
    own = pl.ds(role * SHARE, SHARE)

    def near(other):
        spot_of = lax.rem(other + BLOCKS * core, NEAR)
        return {"aux": (spot_of // BLOCKS) * Z + block * BLOCKS + lax.rem(spot_of, BLOCKS)}

    def far(d):
        return {"aux": side * Z + lax.rem(block + d, BLOCKS) * BLOCKS + place}

    def mate(d):
        other = lax.rem(spot + d, OCC_WAYS * VIR_WAYS)
        return {"occ": other // VIR_WAYS, "vir": lax.rem(other, VIR_WAYS)}

    peers = [near(lax.rem(role + d, NEAR)) for d in range(1, NEAR)]
    crosses = [far(d) for d in range(1, BLOCKS)]
    mates = [mate(d) for d in range(1, OCC_WAYS * VIR_WAYS)]

    loads = [
        pltpu.make_async_copy(start_hbm, start, in_sem.at[0]),
        pltpu.make_async_copy(occ_hbm, eocc, in_sem.at[1]),
        pltpu.make_async_copy(vir_hbm, evir, in_sem.at[2]),
    ]
    fac_loads = [
        pltpu.make_async_copy(
            fac_hbm.at[:, pl.ds(GROUP * c, GROUP)], fac.at[:, pl.ds(GROUP * c, GROUP)], fac_sem.at[c]
        )
        for c in range(ROWS // GROUP)
    ]
    for load in loads + fac_loads:
        load.start()

    barrier = pltpu.get_barrier_semaphore()

    greeted = mates + peers + crosses
    for device in greeted:
        pl.semaphore_signal(barrier, inc=1, device_id=device, device_id_type=MESH)

    for load in loads:
        load.wait()

    def delta(i):
        return evir[...] - eocc[i]

    def contract(source, waits):
        sums = [None, None]
        for i in range(0, ROWS, 2):
            if waits and i % GROUP == 0:
                fac_loads[i // GROUP].wait()
            left = jnp.concatenate([split(source[i]), split(source[i + 1])], axis=1)
            for s in range(2):
                right = jnp.concatenate([fac[s, i], fac[s, i + 1]], axis=1)
                term = lax.dot_general(
                    left, right, (((1,), (1,)), ((), ())), preferred_element_type=f32
                )
                sums[s] = term if sums[s] is None else sums[s] + term
        return [merge(sums[s])[:, LANES * h:LANES * (h + 1)] for s in range(2) for h in range(2)]

    def wait_bytes(ref, sem):
        pltpu.make_async_copy(ref, ref, sem).wait()

    def sum_group(step, tiles, first):
        for index, value in enumerate(tiles):
            cm[step, spot, index] = value
        if first:
            pl.semaphore_wait(barrier, len(greeted))
        for device in mates:
            send(cm.at[step, spot], cm.at[step, spot], (cm_send.at[step], cm_recv.at[step]), device)
        wait_bytes(cm.at[step, pl.ds(0, len(mates))], cm_recv.at[step])
        out = []
        for index in range(len(tiles)):
            sums = [cm[step, j, index] for j in range(OCC_WAYS * VIR_WAYS)]
            while len(sums) > 1:
                sums = [a + b for a, b in zip(sums[0::2], sums[1::2])]
            out.append(sums[0])
        return out

    def send(source, target, sems, device):
        pltpu.make_async_remote_copy(
            src_ref=source, dst_ref=target, send_sem=sems[0], recv_sem=sems[1],
            device_id=device, device_id_type=MESH,
        ).start()

    def scatter(step):
        for d in range(1, NEAR):
            other = lax.rem(role + d, NEAR)

            @pl.when(other < OWNERS)
            def _():
                send(
                    part.at[step, pl.ds(other * SHARE, SHARE)], rs.at[step, role],
                    (rs_send.at[step], rs_recv.at[step]), peers[d - 1],
                )

        @pl.when(owner)
        def _():
            rs[step, role] = part[step, own]

    def back(step, sums):
        scaled = [
            split(jnp.concatenate([2.0 * sums[0], 2.0 * sums[1]], axis=1)),
            split(jnp.concatenate([-sums[2], -sums[3]], axis=1)),
        ]
        for i in range(0, ROWS, 2):
            both = None
            for s in range(2):
                right = jnp.concatenate([fac[s, i], fac[s, i + 1]], axis=1)
                term = lax.dot_general(
                    scaled[s], right, (((1,), (0,)), ((), ())), preferred_element_type=f32
                )
                both = term if both is None else both + term
            both = merge(both)
            part[step, i] = both[:, :LANES]
            part[step, i + 1] = both[:, LANES:]
        scatter(step)

    def spread(step, lower, turned, extra):
        @pl.when(owner)
        def _():
            wait_bytes(rs.at[step, pl.ds(0, NEAR - 1)], rs_recv.at[step])
            sums = [rs[step, j] for j in range(NEAR)]
            while len(sums) > 1:
                sums = [a + b for a, b in zip(sums[0::2], sums[1::2])]
            cx[step, block] = sums[0]
            for d in range(1, BLOCKS):
                send(
                    cx.at[step, block], cx.at[step, block],
                    (cx_send.at[step], cx_recv.at[step]), crosses[d - 1],
                )
            wait_bytes(cx.at[step, pl.ds(0, BLOCKS - 1)], cx_recv.at[step])
            total = (cx[step, 0] + cx[step, 1]) + (cx[step, 2] + cx[step, 3])
            for k in range(SHARE - 1):
                ag[step, role * SHARE + k] = apply(lower, total[k], NV)
            last = role * SHARE + SHARE - 1

            @pl.when(role < OWNERS - 1)
            def _():
                ag[step, last] = apply(lower, total[SHARE - 1], NV)

            @pl.when(role == OWNERS - 1)
            def _():
                half = apply(lower, (total[SHARE - 1] + extra) * (1.0 / PAIRS), NV)
                whole = apply(half, turned)
                ag[step, last] = jnp.where(lane < NV, whole, half)

            for device in peers:
                send(
                    ag.at[step, own], ag.at[step, own],
                    (ag_send.at[step], ag_recv.at[step]), device,
                )
            wait_bytes(ag.at[step, pl.ds(0, TILES - SHARE)], ag_recv.at[step])

        @pl.when(jnp.logical_not(owner))
        def _():
            wait_bytes(ag.at[step], ag_recv.at[step])

    def small(left, right):
        return lax.dot_general(
            left, right, (((1,), (1,)), ((), ())),
            precision=lax.Precision.HIGHEST, preferred_element_type=f32,
        )

    def wide(value):
        return jnp.concatenate(
            [value, jnp.zeros((value.shape[0], LANES - value.shape[1]), f32)], axis=1
        )

    row, lane = iotas()
    weights = [2.0, 2.0, -1.0, -1.0]

    def turn(lower):
        return wide(small(jnp.where(lane == row, 1.0, 0.0)[:, :NV], lower[:, NV:2 * NV]))

    vecs = [start[i] for i in range(ROWS)]
    shifted = [vecs[i] * delta(i) for i in range(ROWS)]
    grams = columns(products(vecs, vecs) + products(vecs, shifted))
    sums = contract(vecs, True)
    *sums, grams = sum_group(0, sums + [grams], True)
    part[0, ROWS] = columns(products([w * v for w, v in zip(weights, sums)], sums))
    back(0, sums)
    lower = factor(grams * (1.0 / PAIRS))
    for index in range(4):
        xhat[index] = apply(lower, sums[index], NV)
    for i in range(ROWS):
        q1[i] = apply(lower, start[i], NV)
    extra = jnp.where(lane < NV, pltpu.roll(grams, LANES - NV, 1), 0.0)
    spread(0, lower, turn(lower), extra)
    proj = ag[0, ROWS]
    coef_ref[0] = proj
    for i in range(ROWS):
        r1[i] = ag[0, i] + delta(i) * q1[i] - apply(proj, q1[i])

    vecs = [r1[i] for i in range(ROWS)]
    moved = [delta(i) * q1[i] for i in range(ROWS)]
    shifted = [vecs[i] * delta(i) for i in range(ROWS)]
    grams = columns(products(vecs, vecs) + products(vecs, shifted) + products(vecs, moved))
    sums = contract(vecs, False)
    *sums, grams = sum_group(1, sums + [grams], False)
    scaled = [w * v for w, v in zip(weights, sums)]
    part[1, ROWS] = columns(products(scaled, sums) + products(scaled, [xhat[k] for k in range(4)]))
    back(1, sums)
    lower = factor(grams * (1.0 / PAIRS))
    coef_ref[1] = jnp.where(lane >= row, lower, 0.0)
    for i in range(ROWS):
        q2[i] = apply(lower, r1[i], NV)
    extra = jnp.where(lane < 2 * NV, pltpu.roll(grams, LANES - NV, 1), 0.0)
    spread(1, lower, turn(lower), extra)
    proj = ag[1, ROWS]
    coef_ref[2] = proj
    for i in range(ROWS):
        resid_ref[i] = ag[1, i] + delta(i) * q2[i] - apply(proj, q2[i]) - apply(proj, q1[i], NV)

    vecs = [resid_ref[i] for i in range(ROWS)]
    gm[spot] = columns(products(vecs, vecs))

    for device in mates:
        send(gm.at[spot], gm.at[spot], (g_send, g_recv), device)
    wait_bytes(gm.at[pl.ds(0, OCC_WAYS * VIR_WAYS - 1)], g_recv)
    sums = [gm[j] for j in range(OCC_WAYS * VIR_WAYS)]
    while len(sums) > 1:
        sums = [a + b for a, b in zip(sums[0::2], sums[1::2])]
    coef_ref[3] = sums[0] * (1.0 / PAIRS)

    for step in range(2):
        wait_bytes(cm.at[step, pl.ds(0, len(mates))], cm_send.at[step])

        @pl.when(owner)
        def _():
            wait_bytes(part.at[step, pl.ds(0, TILES - SHARE)], rs_send.at[step])
            wait_bytes(cx.at[step, pl.ds(0, BLOCKS - 1)], cx_send.at[step])
            wait_bytes(rs.at[step, pl.ds(0, NEAR - 1)], ag_send.at[step])

        @pl.when(jnp.logical_not(owner))
        def _():
            wait_bytes(part.at[step], rs_send.at[step])

    wait_bytes(gm.at[pl.ds(0, OCC_WAYS * VIR_WAYS - 1)], g_send)


def finish(small_ref, resid_ref, coef_ref, next_ref):
    row, lane = iotas()
    lower = factor(small_ref[3])
    for k in range(3):
        coef_ref[k] = small_ref[k][:, :NV]
    coef_ref[3] = jnp.where(lane >= row, lower, 0.0)[:, :NV]
    for i in range(ROWS):
        next_ref[i] = apply(lower, resid_ref[i], NV)


def on_device(start_block, factors, eps_occ, eps_vir):
    tile_shape = (NV, LANES)
    dma = pltpu.SemaphoreType.DMA
    anywhere = pl.BlockSpec(memory_space=pltpu.MemorySpace.HBM)
    vmem = pl.BlockSpec(memory_space=pltpu.MemorySpace.VMEM)
    small, resid = pl.pallas_call(
        kernel,
        out_shape=(
            pltpu.VMEM((4,) + tile_shape, f32),
            pltpu.VMEM((ROWS,) + tile_shape, f32),
        ),
        in_specs=[anywhere] * 4,
        out_specs=(vmem, vmem),
        scratch_shapes=[
            pltpu.VMEM((ROWS,) + tile_shape, f32),
            pltpu.VMEM((2, ROWS, DEPTH, LANES), bf16),
            pltpu.SMEM((ROWS,), f32),
            pltpu.VMEM((1, LANES), f32),
            pltpu.VMEM((ROWS,) + tile_shape, f32),
            pltpu.VMEM((ROWS,) + tile_shape, f32),
            pltpu.VMEM((ROWS,) + tile_shape, f32),
            pltpu.VMEM((4,) + tile_shape, f32),
            pltpu.VMEM((2, OCC_WAYS * VIR_WAYS, 5) + tile_shape, f32),
            pltpu.VMEM((2, TILES) + tile_shape, f32),
            pltpu.VMEM((2, NEAR, SHARE) + tile_shape, f32),
            pltpu.VMEM((2, BLOCKS, SHARE) + tile_shape, f32),
            pltpu.VMEM((2, TILES) + tile_shape, f32),
            pltpu.VMEM((OCC_WAYS * VIR_WAYS,) + tile_shape, f32),
            dma((3,)), dma((ROWS // GROUP,)),
            dma((2,)), dma((2,)),
            dma((2,)), dma((2,)), dma((2,)), dma((2,)), dma((2,)), dma((2,)),
            dma, dma,
        ],
        compiler_params=pltpu.CompilerParams(
            collective_id=0, has_side_effects=True, vmem_limit_bytes=60 * 1024 * 1024
        ),
        cost_estimate=pl.CostEstimate(flops=200_000_000, bytes_accessed=3_000_000, transcendentals=0),
    )(
        start_block.transpose(1, 0, 2),
        factors.transpose(0, 2, 1, 3),
        eps_occ,
        eps_vir.reshape(1, LANES),
    )
    coefs, block = pl.pallas_call(
        finish,
        out_shape=(
            jax.ShapeDtypeStruct((4, NV, NV), f32),
            jax.ShapeDtypeStruct((ROWS,) + tile_shape, f32),
        ),
        in_specs=[vmem] * 2,
        out_specs=(vmem, vmem),
        compiler_params=pltpu.CompilerParams(vmem_limit_bytes=4 * 1024 * 1024),
        cost_estimate=pl.CostEstimate(flops=400_000, bytes_accessed=200_000, transcendentals=0),
    )(small, resid)
    return coefs, block.transpose(1, 0, 2)


def solution(mesh):
    placed = (P(None, "occ", "vir"), P(None, "aux", "occ", "vir"), P("occ"), P("vir"))
    return jax.shard_map(
        on_device,
        mesh=mesh,
        in_specs=placed,
        out_specs=(P(), P(None, "occ", "vir")),
        check_vma=False,
    )
```

```python
import jax
import jax.numpy as jnp
from jax import lax
from jax.experimental import pallas as pl
from jax.experimental.pallas import tpu as pltpu
from jax.sharding import PartitionSpec as P

OCC_WAYS, VIR_WAYS = 4, 4
NV, ROWS, LANES, DEPTH = 8, 20, 128, 256
PAIRS = 40960
TILES = ROWS + 1
AUX_WAYS, Z, SHARE = 32, 16, 3
OWNERS = TILES // SHARE
GROUP = 4
MESH = pl.DeviceIdType.MESH
f32, bf16 = jnp.float32, jnp.bfloat16


def split(value):
    high = value.astype(bf16)
    low = (value - high.astype(f32)).astype(bf16)
    return jnp.concatenate([high, low], axis=0)


def merge(value):
    return value[:NV] + value[NV:]


def apply(matrix, value, first=0):
    total = matrix[:, first:first + 1] * value[0:1, :]
    for m in range(1, NV):
        total = total + matrix[:, first + m:first + m + 1] * value[m:m + 1, :]
    return total


def iotas():
    return (
        lax.broadcasted_iota(jnp.int32, (NV, LANES), 0),
        lax.broadcasted_iota(jnp.int32, (NV, LANES), 1),
    )


def factor(gram):
    row, lane = iotas()
    work = jnp.where(lane < NV, gram, jnp.where(lane == row + NV, 1.0, 0.0))
    scale = jnp.ones((NV, 1), f32)
    rows1 = lax.broadcasted_iota(jnp.int32, (NV, 1), 0)
    for k in range(NV):
        pivot = work[k:k + 1, k:k + 1]
        scale = jnp.where(rows1 == k, pivot, scale)
        if k < NV - 1:
            ratio = jnp.where(rows1 > k, work[:, k:k + 1] / pivot, 0.0)
            work = work - ratio * work[k:k + 1, :]
    return work * (1.0 / jnp.sqrt(scale))


def columns(sums):
    _, lane = iotas()
    out = jnp.zeros((NV, LANES), f32)
    for m, value in enumerate(sums):
        out = jnp.where(lane == m, jnp.sum(value, axis=1, keepdims=True), out)
    return out


def products(lefts, rights):
    sums = []
    for m in range(NV):
        total = lefts[0] * rights[0][m:m + 1, :]
        for left, right in zip(lefts[1:], rights[1:]):
            total = total + left * right[m:m + 1, :]
        sums.append(total)
    return sums


def kernel(
    start_hbm, fac_hbm, occ_hbm, vir_hbm,
    coef_ref, resid_ref,
    start, fac, eocc, evir, q1, q2, r1, xhat,
    cm, part, rs, ag, gm,
    in_sem, fac_sem, cm_send, cm_recv,
    rs_send, rs_recv, ag_send, ag_recv, g_send, g_recv,
):
    aux = lax.axis_index("aux")
    occ = lax.axis_index("occ")
    vir = lax.axis_index("vir")
    spot = occ * VIR_WAYS + vir
    core = lax.rem(vir, 2)

    def owner_of(role):
        return lax.rem(role + core, 2) * Z + 2 * role + core

    depth = lax.rem(aux, Z)
    role = depth // 2
    owner = jnp.logical_and(role < OWNERS, owner_of(role) == aux)
    own = pl.ds(role * SHARE, SHARE)

    def mate(d):
        other = lax.rem(spot + d, OCC_WAYS * VIR_WAYS)
        return {"occ": other // VIR_WAYS, "vir": lax.rem(other, VIR_WAYS)}

    ahead = [lax.rem(aux + d, AUX_WAYS) for d in range(1, AUX_WAYS)]
    ahead = [ahead[k // 2 if k % 2 == 0 else -1 - k // 2] for k in range(AUX_WAYS - 1)]
    owners = [owner_of(r) for r in range(OWNERS)]
    mates = [mate(d) for d in range(1, OCC_WAYS * VIR_WAYS)]

    loads = [
        pltpu.make_async_copy(start_hbm, start, in_sem.at[0]),
        pltpu.make_async_copy(occ_hbm, eocc, in_sem.at[1]),
        pltpu.make_async_copy(vir_hbm, evir, in_sem.at[2]),
    ]
    fac_loads = [
        pltpu.make_async_copy(
            fac_hbm.at[:, pl.ds(GROUP * c, GROUP)], fac.at[:, pl.ds(GROUP * c, GROUP)], fac_sem.at[c]
        )
        for c in range(ROWS // GROUP)
    ]
    for load in loads:
        load.start()

    barrier = pltpu.get_barrier_semaphore()

    def greet(device):
        pl.semaphore_signal(barrier, inc=1, device_id=device, device_id_type=MESH)

    for device in mates:
        greet(device)
    for load in fac_loads:
        load.start()

    @pl.when(owner)
    def _():
        for other in ahead:
            greet({"aux": other})

    @pl.when(jnp.logical_not(owner))
    def _():
        for other in owners:
            greet({"aux": other})

    for load in loads:
        load.wait()

    def delta(i):
        return evir[...] - eocc[i]

    def contract(source, waits):
        sums = [None, None]
        for i in range(0, ROWS, 2):
            if waits and i % GROUP == 0:
                fac_loads[i // GROUP].wait()
            left = jnp.concatenate([split(source[i]), split(source[i + 1])], axis=1)
            for s in range(2):
                right = jnp.concatenate([fac[s, i], fac[s, i + 1]], axis=1)
                term = lax.dot_general(
                    left, right, (((1,), (1,)), ((), ())), preferred_element_type=f32
                )
                sums[s] = term if sums[s] is None else sums[s] + term
        return [merge(sums[s])[:, LANES * h:LANES * (h + 1)] for s in range(2) for h in range(2)]

    def wait_bytes(ref, sem):
        pltpu.make_async_copy(ref, ref, sem).wait()

    def sum_group(step, tiles, first):
        for index, value in enumerate(tiles):
            cm[step, spot, index] = value
        if first:
            @pl.when(owner)
            def _():
                pl.semaphore_wait(barrier, len(mates) + len(ahead))

            @pl.when(jnp.logical_not(owner))
            def _():
                pl.semaphore_wait(barrier, len(mates) + len(owners))

        for device in mates:
            send(cm.at[step, spot], cm.at[step, spot], (cm_send.at[step], cm_recv.at[step]), device)
        wait_bytes(cm.at[step, pl.ds(0, len(mates))], cm_recv.at[step])
        out = []
        for index in range(len(tiles)):
            sums = [cm[step, j, index] for j in range(OCC_WAYS * VIR_WAYS)]
            while len(sums) > 1:
                sums = [a + b for a, b in zip(sums[0::2], sums[1::2])]
            out.append(sums[0])
        return out

    def send(source, target, sems, device):
        pltpu.make_async_remote_copy(
            src_ref=source, dst_ref=target, send_sem=sems[0], recv_sem=sems[1],
            device_id=device, device_id_type=MESH,
        ).start()

    def scatter(step):
        for k in range(OWNERS):
            other = lax.rem(aux + k, OWNERS)
            target = owner_of(other)

            @pl.when(target != aux)
            def _():
                send(
                    part.at[step, pl.ds(other * SHARE, SHARE)], rs.at[step, aux],
                    (rs_send.at[step], rs_recv.at[step]), {"aux": target},
                )

        @pl.when(owner)
        def _():
            rs[step, aux] = part[step, own]

    def back(step, sums):
        scaled = [
            split(jnp.concatenate([2.0 * sums[0], 2.0 * sums[1]], axis=1)),
            split(jnp.concatenate([-sums[2], -sums[3]], axis=1)),
        ]
        for i in range(0, ROWS, 2):
            both = None
            for s in range(2):
                right = jnp.concatenate([fac[s, i], fac[s, i + 1]], axis=1)
                term = lax.dot_general(
                    scaled[s], right, (((1,), (0,)), ((), ())), preferred_element_type=f32
                )
                both = term if both is None else both + term
            both = merge(both)
            part[step, i] = both[:, :LANES]
            part[step, i + 1] = both[:, LANES:]
        scatter(step)

    def spread(step, lower, turned, extra):
        @pl.when(owner)
        def _():
            wait_bytes(rs.at[step, pl.ds(0, AUX_WAYS - 1)], rs_recv.at[step])
            sums = [rs[step, j] for j in range(AUX_WAYS)]
            while len(sums) > 1:
                sums = [a + b for a, b in zip(sums[0::2], sums[1::2])]
            total = sums[0]
            for k in range(SHARE - 1):
                ag[step, role * SHARE + k] = apply(lower, total[k], NV)
            last = role * SHARE + SHARE - 1

            @pl.when(role < OWNERS - 1)
            def _():
                ag[step, last] = apply(lower, total[SHARE - 1], NV)

            @pl.when(role == OWNERS - 1)
            def _():
                half = apply(lower, (total[SHARE - 1] + extra) * (1.0 / PAIRS), NV)
                whole = apply(half, turned)
                ag[step, last] = jnp.where(lane < NV, whole, half)

            for other in ahead:
                send(
                    ag.at[step, own], ag.at[step, own],
                    (ag_send.at[step], ag_recv.at[step]), {"aux": other},
                )
            wait_bytes(ag.at[step, pl.ds(0, TILES - SHARE)], ag_recv.at[step])

        @pl.when(jnp.logical_not(owner))
        def _():
            wait_bytes(ag.at[step], ag_recv.at[step])

    def small(left, right):
        return lax.dot_general(
            left, right, (((1,), (1,)), ((), ())),
            precision=lax.Precision.HIGHEST, preferred_element_type=f32,
        )

    def wide(value):
        return jnp.concatenate(
            [value, jnp.zeros((value.shape[0], LANES - value.shape[1]), f32)], axis=1
        )

    row, lane = iotas()
    weights = [2.0, 2.0, -1.0, -1.0]

    def turn(lower):
        return wide(small(jnp.where(lane == row, 1.0, 0.0)[:, :NV], lower[:, NV:2 * NV]))

    vecs = [start[i] for i in range(ROWS)]
    shifted = [vecs[i] * delta(i) for i in range(ROWS)]
    grams = columns(products(vecs, vecs) + products(vecs, shifted))
    sums = contract(vecs, True)
    *sums, grams = sum_group(0, sums + [grams], True)
    part[0, ROWS] = columns(products([w * v for w, v in zip(weights, sums)], sums))
    back(0, sums)
    lower = factor(grams * (1.0 / PAIRS))
    for index in range(4):
        xhat[index] = apply(lower, sums[index], NV)
    for i in range(ROWS):
        q1[i] = apply(lower, start[i], NV)
    extra = jnp.where(lane < NV, pltpu.roll(grams, LANES - NV, 1), 0.0)
    spread(0, lower, turn(lower), extra)
    proj = ag[0, ROWS]
    coef_ref[0] = proj
    for i in range(ROWS):
        r1[i] = ag[0, i] + delta(i) * q1[i] - apply(proj, q1[i])

    vecs = [r1[i] for i in range(ROWS)]
    moved = [delta(i) * q1[i] for i in range(ROWS)]
    shifted = [vecs[i] * delta(i) for i in range(ROWS)]
    grams = columns(products(vecs, vecs) + products(vecs, shifted) + products(vecs, moved))
    sums = contract(vecs, False)
    *sums, grams = sum_group(1, sums + [grams], False)
    scaled = [w * v for w, v in zip(weights, sums)]
    part[1, ROWS] = columns(products(scaled, sums) + products(scaled, [xhat[k] for k in range(4)]))
    back(1, sums)
    lower = factor(grams * (1.0 / PAIRS))
    coef_ref[1] = jnp.where(lane >= row, lower, 0.0)
    for i in range(ROWS):
        q2[i] = apply(lower, r1[i], NV)
    extra = jnp.where(lane < 2 * NV, pltpu.roll(grams, LANES - NV, 1), 0.0)
    spread(1, lower, turn(lower), extra)
    proj = ag[1, ROWS]
    coef_ref[2] = proj
    for i in range(ROWS):
        resid_ref[i] = ag[1, i] + delta(i) * q2[i] - apply(proj, q2[i]) - apply(proj, q1[i], NV)

    vecs = [resid_ref[i] for i in range(ROWS)]
    gm[spot] = columns(products(vecs, vecs))

    for device in mates:
        send(gm.at[spot], gm.at[spot], (g_send, g_recv), device)
    wait_bytes(gm.at[pl.ds(0, OCC_WAYS * VIR_WAYS - 1)], g_recv)
    sums = [gm[j] for j in range(OCC_WAYS * VIR_WAYS)]
    while len(sums) > 1:
        sums = [a + b for a, b in zip(sums[0::2], sums[1::2])]
    coef_ref[3] = sums[0] * (1.0 / PAIRS)

    for step in range(2):
        wait_bytes(cm.at[step, pl.ds(0, len(mates))], cm_send.at[step])

        @pl.when(owner)
        def _():
            wait_bytes(part.at[step, pl.ds(0, TILES - SHARE)], rs_send.at[step])
            wait_bytes(rs.at[step, pl.ds(0, AUX_WAYS - 1)], ag_send.at[step])

        @pl.when(jnp.logical_not(owner))
        def _():
            wait_bytes(part.at[step], rs_send.at[step])

    wait_bytes(gm.at[pl.ds(0, OCC_WAYS * VIR_WAYS - 1)], g_send)


def finish(small_ref, resid_ref, coef_ref, next_ref):
    row, lane = iotas()
    lower = factor(small_ref[3])
    for k in range(3):
        coef_ref[k] = small_ref[k][:, :NV]
    coef_ref[3] = jnp.where(lane >= row, lower, 0.0)[:, :NV]
    for i in range(ROWS):
        next_ref[i] = apply(lower, resid_ref[i], NV)


def on_device(start_block, factors, eps_occ, eps_vir):
    tile_shape = (NV, LANES)
    dma = pltpu.SemaphoreType.DMA
    anywhere = pl.BlockSpec(memory_space=pltpu.MemorySpace.HBM)
    vmem = pl.BlockSpec(memory_space=pltpu.MemorySpace.VMEM)
    small, resid = pl.pallas_call(
        kernel,
        out_shape=(
            pltpu.VMEM((4,) + tile_shape, f32),
            pltpu.VMEM((ROWS,) + tile_shape, f32),
        ),
        in_specs=[anywhere] * 4,
        out_specs=(vmem, vmem),
        scratch_shapes=[
            pltpu.VMEM((ROWS,) + tile_shape, f32),
            pltpu.VMEM((2, ROWS, DEPTH, LANES), bf16),
            pltpu.SMEM((ROWS,), f32),
            pltpu.VMEM((1, LANES), f32),
            pltpu.VMEM((ROWS,) + tile_shape, f32),
            pltpu.VMEM((ROWS,) + tile_shape, f32),
            pltpu.VMEM((ROWS,) + tile_shape, f32),
            pltpu.VMEM((4,) + tile_shape, f32),
            pltpu.VMEM((2, OCC_WAYS * VIR_WAYS, 5) + tile_shape, f32),
            pltpu.VMEM((2, TILES) + tile_shape, f32),
            pltpu.VMEM((2, AUX_WAYS, SHARE) + tile_shape, f32),
            pltpu.VMEM((2, TILES) + tile_shape, f32),
            pltpu.VMEM((OCC_WAYS * VIR_WAYS,) + tile_shape, f32),
            dma((3,)), dma((ROWS // GROUP,)),
            dma((2,)), dma((2,)),
            dma((2,)), dma((2,)), dma((2,)), dma((2,)),
            dma, dma,
        ],
        compiler_params=pltpu.CompilerParams(
            collective_id=0, has_side_effects=True, vmem_limit_bytes=60 * 1024 * 1024
        ),
        cost_estimate=pl.CostEstimate(flops=200_000_000, bytes_accessed=3_000_000, transcendentals=0),
    )(
        start_block.transpose(1, 0, 2),
        factors.transpose(0, 2, 1, 3),
        eps_occ,
        eps_vir.reshape(1, LANES),
    )
    coefs, block = pl.pallas_call(
        finish,
        out_shape=(
            jax.ShapeDtypeStruct((4, NV, NV), f32),
            jax.ShapeDtypeStruct((ROWS,) + tile_shape, f32),
        ),
        in_specs=[vmem] * 2,
        out_specs=(vmem, vmem),
        compiler_params=pltpu.CompilerParams(vmem_limit_bytes=4 * 1024 * 1024),
        cost_estimate=pl.CostEstimate(flops=400_000, bytes_accessed=200_000, transcendentals=0),
    )(small, resid)
    return coefs, block.transpose(1, 0, 2)


def solution(mesh):
    placed = (P(None, "occ", "vir"), P(None, "aux", "occ", "vir"), P("occ"), P("vir"))
    return jax.shard_map(
        on_device,
        mesh=mesh,
        in_specs=placed,
        out_specs=(P(), P(None, "occ", "vir")),
        check_vma=False,
    )
```

```python
import jax
import jax.numpy as jnp
from jax import lax
from jax.experimental import pallas as pl
from jax.experimental.pallas import tpu as pltpu
from jax.sharding import PartitionSpec as P

OCC_WAYS, VIR_WAYS = 4, 4
NV, ROWS, LANES, DEPTH = 8, 20, 128, 256
PAIRS = 40960
NEAR, BLOCKS, Z = 8, 4, 16
CHUNK = 21
SHIFT = 0
GROUP = 4
MESH = pl.DeviceIdType.MESH
f32, bf16 = jnp.float32, jnp.bfloat16


def split(value):
    high = value.astype(bf16)
    low = (value - high.astype(f32)).astype(bf16)
    return jnp.concatenate([high, low], axis=0)


def merge(value):
    return value[:NV] + value[NV:]


def apply(matrix, value, first=0):
    total = matrix[:, first:first + 1] * value[0:1, :]
    for m in range(1, NV):
        total = total + matrix[:, first + m:first + m + 1] * value[m:m + 1, :]
    return total


def iotas():
    return (
        lax.broadcasted_iota(jnp.int32, (NV, LANES), 0),
        lax.broadcasted_iota(jnp.int32, (NV, LANES), 1),
    )


def factor(gram):
    row, lane = iotas()
    work = jnp.where(lane < NV, gram, jnp.where(lane == row + NV, 1.0, 0.0))
    scale = jnp.ones((NV, 1), f32)
    rows1 = lax.broadcasted_iota(jnp.int32, (NV, 1), 0)
    for k in range(NV):
        pivot = work[k:k + 1, k:k + 1]
        scale = jnp.where(rows1 == k, pivot, scale)
        if k < NV - 1:
            ratio = jnp.where(rows1 > k, work[:, k:k + 1] / pivot, 0.0)
            work = work - ratio * work[k:k + 1, :]
    return work * (1.0 / jnp.sqrt(scale))


def columns(sums):
    _, lane = iotas()
    out = jnp.zeros((NV, LANES), f32)
    for m, value in enumerate(sums):
        out = jnp.where(lane == m, jnp.sum(value, axis=1, keepdims=True), out)
    return out


def products(lefts, rights):
    sums = []
    for m in range(NV):
        total = lefts[0] * rights[0][m:m + 1, :]
        for left, right in zip(lefts[1:], rights[1:]):
            total = total + left * right[m:m + 1, :]
        sums.append(total)
    return sums


def kernel(
    start_hbm, fac_hbm, occ_hbm, vir_hbm,
    coef_ref, resid_ref,
    start, fac, eocc, evir, q1, q2, r1, xhat,
    cm, part, rs, cx, ag, gm,
    in_sem, fac_sem, cm_send, cm_recv,
    rs_send, rs_recv, cx_send, cx_recv, ag_send, ag_recv, g_send, g_recv,
):
    aux = lax.axis_index("aux")
    occ = lax.axis_index("occ")
    vir = lax.axis_index("vir")
    spot = occ * VIR_WAYS + vir
    core = lax.rem(vir, 2)
    side = aux // Z
    along = lax.rem(lax.rem(aux, Z) + SHIFT * core, Z)
    block = along // BLOCKS
    place = lax.rem(along, BLOCKS)
    role = side * BLOCKS + place

    def at(side_of, block_of, place_of):
        back_along = lax.rem(block_of * BLOCKS + place_of + Z - SHIFT * core, Z)
        return {"aux": side_of * Z + back_along}

    def near(other):
        return at(other // BLOCKS, block, lax.rem(other, BLOCKS))

    def far(d):
        return at(side, lax.rem(block + d, BLOCKS), place)

    def mate(d):
        other = lax.rem(spot + d, OCC_WAYS * VIR_WAYS)
        return {"occ": other // VIR_WAYS, "vir": lax.rem(other, VIR_WAYS)}

    peers = [near(lax.rem(role + d, NEAR)) for d in range(1, NEAR)]
    crosses = [far(d) for d in range(1, BLOCKS)]
    mates = [mate(d) for d in range(1, OCC_WAYS * VIR_WAYS)]

    loads = [
        pltpu.make_async_copy(start_hbm, start, in_sem.at[0]),
        pltpu.make_async_copy(occ_hbm, eocc, in_sem.at[1]),
        pltpu.make_async_copy(vir_hbm, evir, in_sem.at[2]),
    ]
    fac_loads = [
        pltpu.make_async_copy(
            fac_hbm.at[:, pl.ds(GROUP * c, GROUP)], fac.at[:, pl.ds(GROUP * c, GROUP)], fac_sem.at[c]
        )
        for c in range(ROWS // GROUP)
    ]
    for load in loads:
        load.start()

    barrier = pltpu.get_barrier_semaphore()

    greeted = mates + peers + crosses
    for device in greeted:
        pl.semaphore_signal(barrier, inc=1, device_id=device, device_id_type=MESH)
    for load in fac_loads:
        load.start()

    for load in loads:
        load.wait()

    def delta(i):
        return evir[...] - eocc[i]

    def contract(source, waits):
        sums = [None, None]
        for i in range(0, ROWS, 2):
            if waits and i % GROUP == 0:
                fac_loads[i // GROUP].wait()
            left = jnp.concatenate([split(source[i]), split(source[i + 1])], axis=1)
            for s in range(2):
                right = jnp.concatenate([fac[s, i], fac[s, i + 1]], axis=1)
                term = lax.dot_general(
                    left, right, (((1,), (1,)), ((), ())), preferred_element_type=f32
                )
                sums[s] = term if sums[s] is None else sums[s] + term
        return [merge(sums[s])[:, LANES * h:LANES * (h + 1)] for s in range(2) for h in range(2)]

    def wait_bytes(ref, sem):
        pltpu.make_async_copy(ref, ref, sem).wait()

    def sum_group(step, tiles, first):
        for index, value in enumerate(tiles):
            cm[step, spot, index] = value
        if first:
            pl.semaphore_wait(barrier, len(greeted))
        for device in mates:
            send(cm.at[step, spot], cm.at[step, spot], (cm_send.at[step], cm_recv.at[step]), device)
        wait_bytes(cm.at[step, pl.ds(0, len(mates))], cm_recv.at[step])
        out = []
        for index in range(len(tiles)):
            sums = [cm[step, j, index] for j in range(OCC_WAYS * VIR_WAYS)]
            while len(sums) > 1:
                sums = [a + b for a, b in zip(sums[0::2], sums[1::2])]
            out.append(sums[0])
        return out

    def send(source, target, sems, device):
        pltpu.make_async_remote_copy(
            src_ref=source, dst_ref=target, send_sem=sems[0], recv_sem=sems[1],
            device_id=device, device_id_type=MESH,
        ).start()

    def put(step, i, value):
        j, k = i // 5, i % 5
        if k == 2:
            part[step, 2 * j, 2 * NV:2 * NV + NV // 2] = value[:NV // 2]
            part[step, 2 * j + 1, 2 * NV:2 * NV + NV // 2] = value[NV // 2:]
        else:
            first = NV * (k % 3)
            part[step, 2 * j + k // 3, first:first + NV] = value

    def take(step, i):
        j, k = i // 5, i % 5
        if k == 2:
            return jnp.concatenate(
                [ag[step, 2 * j + h, 2 * NV:2 * NV + NV // 2] for h in range(2)], axis=0
            )
        first = NV * (k % 3)
        return ag[step, 2 * j + k // 3, first:first + NV]

    def put_small(step, value):
        for n in range(NV):
            part[step, n, CHUNK - 1:CHUNK] = value[n:n + 1]

    def take_small(step):
        return jnp.concatenate([ag[step, n, CHUNK - 1:CHUNK] for n in range(NV)], axis=0)

    def scatter(step):
        for d in range(1, NEAR):
            send(
                part.at[step, lax.rem(role + d, NEAR)], rs.at[step, role],
                (rs_send.at[step], rs_recv.at[step]), peers[d - 1],
            )
        rs[step, role] = part[step, role]

    def back(step, sums):
        scaled = [
            split(jnp.concatenate([2.0 * sums[0], 2.0 * sums[1]], axis=1)),
            split(jnp.concatenate([-sums[2], -sums[3]], axis=1)),
        ]
        for i in range(0, ROWS, 2):
            both = None
            for s in range(2):
                right = jnp.concatenate([fac[s, i], fac[s, i + 1]], axis=1)
                term = lax.dot_general(
                    scaled[s], right, (((1,), (0,)), ((), ())), preferred_element_type=f32
                )
                both = term if both is None else both + term
            both = merge(both)
            put(step, i, both[:, :LANES])
            put(step, i + 1, both[:, LANES:])
        scatter(step)

    def spread(step):
        wait_bytes(rs.at[step, pl.ds(0, NEAR - 1)], rs_recv.at[step])
        sums = [rs[step, j] for j in range(NEAR)]
        while len(sums) > 1:
            sums = [a + b for a, b in zip(sums[0::2], sums[1::2])]
        cx[step, block] = sums[0]
        for device in crosses:
            send(cx.at[step, block], cx.at[step, block], (cx_send.at[step], cx_recv.at[step]), device)
        wait_bytes(cx.at[step, pl.ds(0, BLOCKS - 1)], cx_recv.at[step])
        ag[step, role] = (cx[step, 0] + cx[step, 1]) + (cx[step, 2] + cx[step, 3])
        for device in peers:
            send(ag.at[step, role], ag.at[step, role], (ag_send.at[step], ag_recv.at[step]), device)
        wait_bytes(ag.at[step, pl.ds(0, NEAR - 1)], ag_recv.at[step])

    def rotated(lower, turned, value):
        half = apply(lower, value * (1.0 / PAIRS), NV)
        return jnp.where(lane < NV, apply(half, turned), half)

    def small(left, right):
        return lax.dot_general(
            left, right, (((1,), (1,)), ((), ())),
            precision=lax.Precision.HIGHEST, preferred_element_type=f32,
        )

    def wide(value):
        return jnp.concatenate(
            [value, jnp.zeros((value.shape[0], LANES - value.shape[1]), f32)], axis=1
        )

    row, lane = iotas()
    weights = [2.0, 2.0, -1.0, -1.0]

    def turn(lower):
        return wide(small(jnp.where(lane == row, 1.0, 0.0)[:, :NV], lower[:, NV:2 * NV]))

    vecs = [start[i] for i in range(ROWS)]
    shifted = [vecs[i] * delta(i) for i in range(ROWS)]
    grams = columns(products(vecs, vecs) + products(vecs, shifted))
    sums = contract(vecs, True)
    *sums, grams = sum_group(0, sums + [grams], True)
    put_small(0, columns(products([w * v for w, v in zip(weights, sums)], sums)))
    back(0, sums)
    lower = factor(grams * (1.0 / PAIRS))
    for index in range(4):
        xhat[index] = apply(lower, sums[index], NV)
    for i in range(ROWS):
        q1[i] = apply(lower, start[i], NV)
    extra = jnp.where(lane < NV, pltpu.roll(grams, LANES - NV, 1), 0.0)
    turned = turn(lower)
    spread(0)
    proj = rotated(lower, turned, take_small(0) + extra)
    proj1 = proj
    for i in range(ROWS):
        r1[i] = apply(lower, take(0, i), NV) + delta(i) * q1[i] - apply(proj, q1[i])

    vecs = [r1[i] for i in range(ROWS)]
    moved = [delta(i) * q1[i] for i in range(ROWS)]
    shifted = [vecs[i] * delta(i) for i in range(ROWS)]
    grams = columns(products(vecs, vecs) + products(vecs, shifted) + products(vecs, moved))
    sums = contract(vecs, False)
    *sums, grams = sum_group(1, sums + [grams], False)
    scaled = [w * v for w, v in zip(weights, sums)]
    put_small(1, columns(products(scaled, sums) + products(scaled, [xhat[k] for k in range(4)])))
    back(1, sums)
    lower = factor(grams * (1.0 / PAIRS))
    coef_ref[1] = jnp.where(lane >= row, lower, 0.0)
    for i in range(ROWS):
        q2[i] = apply(lower, r1[i], NV)
    extra = jnp.where(lane < 2 * NV, pltpu.roll(grams, LANES - NV, 1), 0.0)
    turned = turn(lower)
    spread(1)
    proj = rotated(lower, turned, take_small(1) + extra)
    for i in range(ROWS):
        resid_ref[i] = (
            apply(lower, take(1, i), NV) + delta(i) * q2[i] - apply(proj, q2[i]) - apply(proj, q1[i], NV)
        )

    vecs = [resid_ref[i] for i in range(ROWS)]
    grams = columns(products(vecs, vecs))
    grams = jnp.where(jnp.logical_and(lane >= NV, lane < 2 * NV), pltpu.roll(proj1, NV, 1), grams)
    grams = jnp.where(
        jnp.logical_and(lane >= 2 * NV, lane < 3 * NV), pltpu.roll(proj, 2 * NV, 1), grams
    )
    gm[spot] = grams

    for device in mates:
        send(gm.at[spot], gm.at[spot], (g_send, g_recv), device)
    wait_bytes(gm.at[pl.ds(0, OCC_WAYS * VIR_WAYS - 1)], g_recv)
    sums = [gm[j] for j in range(OCC_WAYS * VIR_WAYS)]
    while len(sums) > 1:
        sums = [a + b for a, b in zip(sums[0::2], sums[1::2])]
    coef_ref[3] = sums[0] * (1.0 / PAIRS)
    coef_ref[0] = pltpu.roll(gm[0], LANES - NV, 1)
    coef_ref[2] = pltpu.roll(gm[0], LANES - 2 * NV, 1)

    for step in range(2):
        wait_bytes(cm.at[step, pl.ds(0, len(mates))], cm_send.at[step])

        wait_bytes(rs.at[step, pl.ds(0, NEAR - 1)], rs_send.at[step])
        wait_bytes(cx.at[step, pl.ds(0, BLOCKS - 1)], cx_send.at[step])
        wait_bytes(rs.at[step, pl.ds(0, NEAR - 1)], ag_send.at[step])

    wait_bytes(gm.at[pl.ds(0, OCC_WAYS * VIR_WAYS - 1)], g_send)


def finish(small_ref, resid_ref, coef_ref, next_ref):
    row, lane = iotas()
    lower = factor(small_ref[3])
    for k in range(3):
        coef_ref[k] = small_ref[k][:, :NV]
    coef_ref[3] = jnp.where(lane >= row, lower, 0.0)[:, :NV]
    for i in range(ROWS):
        next_ref[i] = apply(lower, resid_ref[i], NV)


def on_device(start_block, factors, eps_occ, eps_vir):
    tile_shape = (NV, LANES)
    dma = pltpu.SemaphoreType.DMA
    anywhere = pl.BlockSpec(memory_space=pltpu.MemorySpace.HBM)
    vmem = pl.BlockSpec(memory_space=pltpu.MemorySpace.VMEM)
    small, resid = pl.pallas_call(
        kernel,
        out_shape=(
            pltpu.VMEM((4,) + tile_shape, f32),
            pltpu.VMEM((ROWS,) + tile_shape, f32),
        ),
        in_specs=[anywhere] * 4,
        out_specs=(vmem, vmem),
        scratch_shapes=[
            pltpu.VMEM((ROWS,) + tile_shape, f32),
            pltpu.VMEM((2, ROWS, DEPTH, LANES), bf16),
            pltpu.SMEM((ROWS,), f32),
            pltpu.VMEM((1, LANES), f32),
            pltpu.VMEM((ROWS,) + tile_shape, f32),
            pltpu.VMEM((ROWS,) + tile_shape, f32),
            pltpu.VMEM((ROWS,) + tile_shape, f32),
            pltpu.VMEM((4,) + tile_shape, f32),
            pltpu.VMEM((2, OCC_WAYS * VIR_WAYS, 5) + tile_shape, f32),
            pltpu.VMEM((2, NEAR, CHUNK, LANES), f32),
            pltpu.VMEM((2, NEAR, CHUNK, LANES), f32),
            pltpu.VMEM((2, BLOCKS, CHUNK, LANES), f32),
            pltpu.VMEM((2, NEAR, CHUNK, LANES), f32),
            pltpu.VMEM((OCC_WAYS * VIR_WAYS,) + tile_shape, f32),
            dma((3,)), dma((ROWS // GROUP,)),
            dma((2,)), dma((2,)),
            dma((2,)), dma((2,)), dma((2,)), dma((2,)), dma((2,)), dma((2,)),
            dma, dma,
        ],
        compiler_params=pltpu.CompilerParams(
            collective_id=0, has_side_effects=True, vmem_limit_bytes=60 * 1024 * 1024
        ),
        cost_estimate=pl.CostEstimate(flops=200_000_000, bytes_accessed=3_000_000, transcendentals=0),
    )(
        start_block.transpose(1, 0, 2),
        factors.transpose(0, 2, 1, 3),
        eps_occ,
        eps_vir.reshape(1, LANES),
    )
    coefs, block = pl.pallas_call(
        finish,
        out_shape=(
            jax.ShapeDtypeStruct((4, NV, NV), f32),
            jax.ShapeDtypeStruct((ROWS,) + tile_shape, f32),
        ),
        in_specs=[vmem] * 2,
        out_specs=(vmem, vmem),
        compiler_params=pltpu.CompilerParams(vmem_limit_bytes=4 * 1024 * 1024),
        cost_estimate=pl.CostEstimate(flops=400_000, bytes_accessed=200_000, transcendentals=0),
    )(small, resid)
    return coefs, block.transpose(1, 0, 2)


def solution(mesh):
    placed = (P(None, "occ", "vir"), P(None, "aux", "occ", "vir"), P("occ"), P("vir"))
    return jax.shard_map(
        on_device,
        mesh=mesh,
        in_specs=placed,
        out_specs=(P(), P(None, "occ", "vir")),
        check_vma=False,
    )
```

```python
import jax
import jax.numpy as jnp
from jax import lax
from jax.experimental import pallas as pl
from jax.experimental.pallas import tpu as pltpu
from jax.sharding import PartitionSpec as P

OCC_WAYS, VIR_WAYS = 4, 4
NV, ROWS, LANES, DEPTH = 8, 20, 128, 256
PAIRS = 40960
TILES = ROWS + 1
NEAR, BLOCKS, Z, SHARE = 8, 4, 16, 3
OWNERS = TILES // SHARE
HALF = ROWS // 2
MESH = pl.DeviceIdType.MESH
f32, bf16 = jnp.float32, jnp.bfloat16


def split(value):
    high = value.astype(bf16)
    low = (value - high.astype(f32)).astype(bf16)
    return jnp.concatenate([high, low], axis=0)


def merge(value):
    return value[:NV] + value[NV:]


def columns_of(matrix, first=0):
    return [
        jnp.broadcast_to(matrix[:, first + m:first + m + 1], (NV, LANES)) for m in range(NV)
    ]


def apply(columns, value):
    total = columns[0] * value[0:1, :]
    for m in range(1, NV):
        total = total + columns[m] * value[m:m + 1, :]
    return total


def iotas():
    return (
        lax.broadcasted_iota(jnp.int32, (NV, LANES), 0),
        lax.broadcasted_iota(jnp.int32, (NV, LANES), 1),
    )


def factor(gram):
    row, lane = iotas()
    work = jnp.where(lane < NV, gram, jnp.where(lane == row + NV, 1.0, 0.0))
    scale = jnp.ones((NV, 1), f32)
    rows1 = lax.broadcasted_iota(jnp.int32, (NV, 1), 0)
    for k in range(NV):
        pivot = work[k:k + 1, k:k + 1]
        scale = jnp.where(rows1 == k, pivot, scale)
        if k < NV - 1:
            ratio = jnp.where(rows1 > k, work[:, k:k + 1] / pivot, 0.0)
            work = work - ratio * work[k:k + 1, :]
    return work * (1.0 / jnp.sqrt(scale))


def columns(sums):
    _, lane = iotas()
    out = jnp.zeros((NV, LANES), f32)
    for m, value in enumerate(sums):
        out = jnp.where(lane == m, jnp.sum(value, axis=1, keepdims=True), out)
    return out


def add_products(sums, lefts, right):
    for m in range(NV):
        row = right[m:m + 1, :]
        for k, left in enumerate(lefts):
            sums[k * NV + m] = sums[k * NV + m] + left * row
    return sums


def zeros(count):
    return [jnp.zeros((NV, LANES), f32) for _ in range(count)]


def kernel(
    start_hbm, fac_hbm, occ_hbm, vir_hbm,
    coef_ref, resid_ref,
    fac, eocc, evir, q,
    cm, part, rs, cx, ag, gm,
    in_sem, fac_sem, cm_send, cm_recv,
    rs_send, rs_recv, cx_send, cx_recv, ag_send, ag_recv, g_send, g_recv,
):
    aux = lax.axis_index("aux")
    occ = lax.axis_index("occ")
    vir = lax.axis_index("vir")
    spot = occ * VIR_WAYS + vir
    core = lax.rem(vir, 2)
    side = aux // Z
    block = lax.rem(aux, Z) // BLOCKS
    place = lax.rem(aux, BLOCKS)
    role = lax.rem(side * BLOCKS + place + BLOCKS * core, NEAR)
    owner = role < OWNERS
    own = pl.ds(role * SHARE, SHARE)

    def near(other):
        spot_of = lax.rem(other + BLOCKS * core, NEAR)
        return {"aux": (spot_of // BLOCKS) * Z + block * BLOCKS + lax.rem(spot_of, BLOCKS)}

    def far(d):
        return {"aux": side * Z + lax.rem(block + d, BLOCKS) * BLOCKS + place}

    def mate(d):
        other = lax.rem(spot + d, OCC_WAYS * VIR_WAYS)
        return {"occ": other // VIR_WAYS, "vir": lax.rem(other, VIR_WAYS)}

    peers = [near(lax.rem(role + d, NEAR)) for d in range(1, NEAR)]
    crosses = [far(d) for d in range(1, BLOCKS)]
    mates = [mate(d) for d in range(1, OCC_WAYS * VIR_WAYS)]

    loads = [
        pltpu.make_async_copy(start_hbm, resid_ref, in_sem.at[0]),
        pltpu.make_async_copy(occ_hbm, eocc, in_sem.at[1]),
        pltpu.make_async_copy(vir_hbm, evir, in_sem.at[2]),
    ]
    fac_loads = [
        pltpu.make_async_copy(
            fac_hbm.at[:, pl.ds(HALF * c, HALF)], fac.at[:, pl.ds(HALF * c, HALF)], fac_sem.at[c]
        )
        for c in range(2)
    ]
    for load in loads:
        load.start()

    barrier = pltpu.get_barrier_semaphore()

    greeted = mates + peers + crosses
    for device in mates:
        pl.semaphore_signal(barrier, inc=1, device_id=device, device_id_type=MESH)
    for load in fac_loads:
        load.start()
    for device in peers + crosses:
        pl.semaphore_signal(barrier, inc=1, device_id=device, device_id_type=MESH)

    for i in range(ROWS):
        q[0, i] = jnp.zeros((NV, LANES), f32)
    for load in loads:
        load.wait()

    def delta(i):
        return evir[...] - eocc[i]

    def pairs(s, i):
        return jnp.concatenate([fac[s, i], fac[s, i + 1]], axis=1)

    def contract(step):
        def body(half, carry):
            @pl.when(step == 0)
            def _():
                pltpu.make_async_copy(
                    fac_hbm.at[:, pl.ds(HALF * half, HALF)], fac.at[:, pl.ds(HALF * half, HALF)],
                    fac_sem.at[half],
                ).wait()

            sums, grams = list(carry[:2]), list(carry[2:])
            for k in range(0, HALF, 2):
                i = half * HALF + k
                left = []
                for u in range(2):
                    value = resid_ref[i + u]
                    shift = delta(i + u)
                    grams = add_products(grams, [value, shift * value, shift * q[step, i + u]], value)
                    left.append(split(value))
                left = jnp.concatenate(left, axis=1)
                for s in range(2):
                    sums[s] = sums[s] + lax.dot_general(
                        left, pairs(s, i), (((1,), (1,)), ((), ())), preferred_element_type=f32
                    )
            return (*sums, *grams)

        start = [jnp.zeros((2 * NV, DEPTH), f32) for _ in range(2)] + zeros(3 * NV)
        out = lax.fori_loop(0, 2, body, tuple(start))
        tiles = [merge(out[s])[:, LANES * h:LANES * (h + 1)] for s in range(2) for h in range(2)]
        return tiles + [columns(out[2:])]

    def wait_bytes(ref, sem):
        pltpu.make_async_copy(ref, ref, sem).wait()

    def sum_group(step, tiles):
        for index, value in enumerate(tiles):
            cm[step, spot, index] = value

        @pl.when(step == 0)
        def _():
            pl.semaphore_wait(barrier, len(greeted))

        for device in mates:
            send(cm.at[step, spot], cm.at[step, spot], (cm_send.at[step], cm_recv.at[step]), device)
        wait_bytes(cm.at[step, pl.ds(0, len(mates))], cm_recv.at[step])
        out = []
        for index in range(len(tiles)):
            sums = [cm[step, j, index] for j in range(OCC_WAYS * VIR_WAYS)]
            while len(sums) > 1:
                sums = [a + b for a, b in zip(sums[0::2], sums[1::2])]
            out.append(sums[0])
        return out

    def send(source, target, sems, device):
        pltpu.make_async_remote_copy(
            src_ref=source, dst_ref=target, send_sem=sems[0], recv_sem=sems[1],
            device_id=device, device_id_type=MESH,
        ).start()

    def scatter(step):
        for d in range(1, NEAR):
            other = lax.rem(role + d, NEAR)

            @pl.when(other < OWNERS)
            def _():
                send(
                    part.at[step, pl.ds(other * SHARE, SHARE)], rs.at[step, role],
                    (rs_send.at[step], rs_recv.at[step]), peers[d - 1],
                )

        @pl.when(owner)
        def _():
            rs[step, role] = part[step, own]

    def back(step, sums):
        scaled = [
            split(jnp.concatenate([2.0 * sums[0], 2.0 * sums[1]], axis=1)),
            split(jnp.concatenate([-sums[2], -sums[3]], axis=1)),
        ]

        def body(half, carry):
            for k in range(0, HALF, 2):
                i = half * HALF + k
                both = None
                for s in range(2):
                    term = lax.dot_general(
                        scaled[s], pairs(s, i), (((1,), (0,)), ((), ())), preferred_element_type=f32
                    )
                    both = term if both is None else both + term
                both = merge(both)
                part[step, i] = both[:, :LANES]
                part[step, i + 1] = both[:, LANES:]
            return carry

        lax.fori_loop(0, 2, body, 0)
        scatter(step)

    def spread(step, lower, turned, extra):
        @pl.when(owner)
        def _():
            wait_bytes(rs.at[step, pl.ds(0, NEAR - 1)], rs_recv.at[step])
            sums = [rs[step, j] for j in range(NEAR)]
            while len(sums) > 1:
                sums = [a + b for a, b in zip(sums[0::2], sums[1::2])]
            cx[step, block] = sums[0]
            for d in range(1, BLOCKS):
                send(
                    cx.at[step, block], cx.at[step, block],
                    (cx_send.at[step], cx_recv.at[step]), crosses[d - 1],
                )
            wait_bytes(cx.at[step, pl.ds(0, BLOCKS - 1)], cx_recv.at[step])
            total = (cx[step, 0] + cx[step, 1]) + (cx[step, 2] + cx[step, 3])
            for k in range(SHARE - 1):
                ag[step, role * SHARE + k] = apply(lower, total[k])
            last = role * SHARE + SHARE - 1

            @pl.when(role < OWNERS - 1)
            def _():
                ag[step, last] = apply(lower, total[SHARE - 1])

            @pl.when(role == OWNERS - 1)
            def _():
                half = apply(lower, (total[SHARE - 1] + extra) * (1.0 / PAIRS))
                whole = apply(columns_of(half), turned)
                ag[step, last] = jnp.where(lane < NV, whole, half)

            for device in peers:
                send(
                    ag.at[step, own], ag.at[step, own],
                    (ag_send.at[step], ag_recv.at[step]), device,
                )
            wait_bytes(ag.at[step, pl.ds(0, TILES - SHARE)], ag_recv.at[step])

        @pl.when(jnp.logical_not(owner))
        def _():
            wait_bytes(ag.at[step], ag_recv.at[step])

    def small(left, right):
        return lax.dot_general(
            left, right, (((1,), (1,)), ((), ())),
            precision=lax.Precision.HIGHEST, preferred_element_type=f32,
        )

    def wide(value):
        return jnp.concatenate(
            [value, jnp.zeros((value.shape[0], LANES - value.shape[1]), f32)], axis=1
        )

    row, lane = iotas()
    weights = [2.0, 2.0, -1.0, -1.0]

    def turned(value):
        return wide(small(jnp.where(lane == row, 1.0, 0.0)[:, :NV], value))

    def one_step(step, hats):
        *sums, grams = sum_group(step, contract(step))
        scaled = [w * v for w, v in zip(weights, sums)]
        pieces = zeros(2 * NV)
        for m in range(NV):
            for k in range(4):
                pieces[m] = pieces[m] + scaled[k] * sums[k][m:m + 1, :]
                pieces[NV + m] = pieces[NV + m] + scaled[k] * hats[k][m:m + 1, :]
        part[step, ROWS] = columns(pieces)
        back(step, sums)

        both = factor(grams * (1.0 / PAIRS))
        coef_ref[lax.rem(2 * step + 3, 4)] = jnp.where(lane >= row, both, 0.0)
        lower = columns_of(both, NV)
        after = tuple(apply(lower, sums[k]) for k in range(4))

        def turn_block(group, carry):
            for k in range(4):
                q[step + 1, group * 4 + k] = apply(lower, resid_ref[group * 4 + k])
            return carry

        lax.fori_loop(0, ROWS // 4, turn_block, 0)
        extra = jnp.where(lane < NV, pltpu.roll(grams, LANES - NV, 1), 0.0)
        extra = extra + pltpu.roll(turned(grams[:, 2 * NV:3 * NV]), NV, 1)
        spread(step, lower, turned(both[:, NV:2 * NV]), extra)

        proj = ag[step, ROWS]
        coef_ref[2 * step] = proj
        now, before = columns_of(proj), columns_of(proj, NV)

        def take_away(half, carry):
            for k in range(HALF):
                i = half * HALF + k
                block = q[step + 1, i]
                resid_ref[i] = (
                    ag[step, i] + delta(i) * block - apply(now, block) - apply(before, q[step, i])
                )
            return carry

        lax.fori_loop(0, 2, take_away, 0)
        return after

    lax.fori_loop(0, 2, one_step, tuple(zeros(4)))

    def last_products(half, sums):
        sums = list(sums)
        for k in range(HALF):
            value = resid_ref[half * HALF + k]
            sums = add_products(sums, [value], value)
        return tuple(sums)

    gm[spot] = columns(lax.fori_loop(0, 2, last_products, tuple(zeros(NV))))

    for device in mates:
        send(gm.at[spot], gm.at[spot], (g_send, g_recv), device)
    wait_bytes(gm.at[pl.ds(0, OCC_WAYS * VIR_WAYS - 1)], g_recv)
    sums = [gm[j] for j in range(OCC_WAYS * VIR_WAYS)]
    while len(sums) > 1:
        sums = [a + b for a, b in zip(sums[0::2], sums[1::2])]
    coef_ref[3] = sums[0] * (1.0 / PAIRS)

    for step in range(2):
        wait_bytes(cm.at[step, pl.ds(0, len(mates))], cm_send.at[step])

        @pl.when(owner)
        def _():
            wait_bytes(part.at[step, pl.ds(0, TILES - SHARE)], rs_send.at[step])
            wait_bytes(cx.at[step, pl.ds(0, BLOCKS - 1)], cx_send.at[step])
            wait_bytes(rs.at[step, pl.ds(0, NEAR - 1)], ag_send.at[step])

        @pl.when(jnp.logical_not(owner))
        def _():
            wait_bytes(part.at[step], rs_send.at[step])

    wait_bytes(gm.at[pl.ds(0, OCC_WAYS * VIR_WAYS - 1)], g_send)


def finish(small_ref, resid_ref, coef_ref, next_ref):
    row, lane = iotas()
    lower = factor(small_ref[3])
    inverse = columns_of(lower, NV)
    for k in range(3):
        coef_ref[k] = small_ref[k][:, :NV]
    coef_ref[3] = jnp.where(lane >= row, lower, 0.0)[:, :NV]
    for i in range(ROWS):
        next_ref[i] = apply(inverse, resid_ref[i])


def on_device(start_block, factors, eps_occ, eps_vir):
    tile_shape = (NV, LANES)
    dma = pltpu.SemaphoreType.DMA
    anywhere = pl.BlockSpec(memory_space=pltpu.MemorySpace.HBM)
    vmem = pl.BlockSpec(memory_space=pltpu.MemorySpace.VMEM)
    small, resid = pl.pallas_call(
        kernel,
        out_shape=(
            pltpu.VMEM((4,) + tile_shape, f32),
            pltpu.VMEM((ROWS,) + tile_shape, f32),
        ),
        in_specs=[anywhere] * 4,
        out_specs=(vmem, vmem),
        scratch_shapes=[
            pltpu.VMEM((2, ROWS, DEPTH, LANES), bf16),
            pltpu.SMEM((ROWS,), f32),
            pltpu.VMEM((1, LANES), f32),
            pltpu.VMEM((3, ROWS) + tile_shape, f32),
            pltpu.VMEM((2, OCC_WAYS * VIR_WAYS, 5) + tile_shape, f32),
            pltpu.VMEM((2, TILES) + tile_shape, f32),
            pltpu.VMEM((2, NEAR, SHARE) + tile_shape, f32),
            pltpu.VMEM((2, BLOCKS, SHARE) + tile_shape, f32),
            pltpu.VMEM((2, TILES) + tile_shape, f32),
            pltpu.VMEM((OCC_WAYS * VIR_WAYS,) + tile_shape, f32),
            dma((3,)), dma((2,)),
            dma((2,)), dma((2,)),
            dma((2,)), dma((2,)), dma((2,)), dma((2,)), dma((2,)), dma((2,)),
            dma, dma,
        ],
        compiler_params=pltpu.CompilerParams(
            collective_id=0, has_side_effects=True, vmem_limit_bytes=60 * 1024 * 1024
        ),
        cost_estimate=pl.CostEstimate(flops=200_000_000, bytes_accessed=3_000_000, transcendentals=0),
    )(
        start_block.transpose(1, 0, 2),
        factors.transpose(0, 2, 1, 3),
        eps_occ,
        eps_vir.reshape(1, LANES),
    )
    coefs, block = pl.pallas_call(
        finish,
        out_shape=(
            jax.ShapeDtypeStruct((4, NV, NV), f32),
            jax.ShapeDtypeStruct((ROWS,) + tile_shape, f32),
        ),
        in_specs=[vmem] * 2,
        out_specs=(vmem, vmem),
        compiler_params=pltpu.CompilerParams(vmem_limit_bytes=4 * 1024 * 1024),
        cost_estimate=pl.CostEstimate(flops=400_000, bytes_accessed=200_000, transcendentals=0),
    )(small, resid)
    return coefs, block.transpose(1, 0, 2)


def solution(mesh):
    placed = (P(None, "occ", "vir"), P(None, "aux", "occ", "vir"), P("occ"), P("vir"))
    return jax.shard_map(
        on_device,
        mesh=mesh,
        in_specs=placed,
        out_specs=(P(), P(None, "occ", "vir")),
        check_vma=False,
    )
```

```python
import jax
import jax.numpy as jnp
from jax import lax
from jax.experimental import pallas as pl
from jax.experimental.pallas import tpu as pltpu
from jax.sharding import PartitionSpec as P

OCC_WAYS, VIR_WAYS = 4, 4
NV, ROWS, LANES, DEPTH = 8, 20, 128, 256
PAIRS = 40960
TILES = ROWS + 1
NEAR, BLOCKS, Z, SHARE = 8, 4, 16, 3
OWNERS = TILES // SHARE
CHIPS = 8
GROUP = 4
MESH = pl.DeviceIdType.MESH
f32, bf16 = jnp.float32, jnp.bfloat16


def split(value):
    high = value.astype(bf16)
    low = (value - high.astype(f32)).astype(bf16)
    return jnp.concatenate([high, low], axis=0)


def merge(value):
    return value[:NV] + value[NV:]


def apply(matrix, value, first=0):
    total = matrix[:, first:first + 1] * value[0:1, :]
    for m in range(1, NV):
        total = total + matrix[:, first + m:first + m + 1] * value[m:m + 1, :]
    return total


def iotas():
    return (
        lax.broadcasted_iota(jnp.int32, (NV, LANES), 0),
        lax.broadcasted_iota(jnp.int32, (NV, LANES), 1),
    )


def factor(gram):
    row, lane = iotas()
    work = jnp.where(lane < NV, gram, jnp.where(lane == row + NV, 1.0, 0.0))
    scale = jnp.ones((NV, 1), f32)
    rows1 = lax.broadcasted_iota(jnp.int32, (NV, 1), 0)
    for k in range(NV):
        pivot = work[k:k + 1, k:k + 1]
        scale = jnp.where(rows1 == k, pivot, scale)
        if k < NV - 1:
            ratio = jnp.where(rows1 > k, work[:, k:k + 1] / pivot, 0.0)
            work = work - ratio * work[k:k + 1, :]
    return work * (1.0 / jnp.sqrt(scale))


def columns(sums):
    _, lane = iotas()
    out = jnp.zeros((NV, LANES), f32)
    for m, value in enumerate(sums):
        out = jnp.where(lane == m, jnp.sum(value, axis=1, keepdims=True), out)
    return out


def products(lefts, rights):
    sums = []
    for m in range(NV):
        total = lefts[0] * rights[0][m:m + 1, :]
        for left, right in zip(lefts[1:], rights[1:]):
            total = total + left * right[m:m + 1, :]
        sums.append(total)
    return sums


def kernel(
    start_hbm, fac_hbm, occ_hbm, vir_hbm,
    coef_ref, resid_ref,
    start, fac, eocc, evir, q1, q2, r1, xhat,
    cc, cm, part, rs, cx, ag, gm,
    in_sem, fac_sem, cc_send, cc_recv, cm_send, cm_recv,
    rs_send, rs_recv, cx_send, cx_recv, ag_send, ag_recv, g_send, g_recv,
):
    aux = lax.axis_index("aux")
    occ = lax.axis_index("occ")
    vir = lax.axis_index("vir")
    spot = occ * VIR_WAYS + vir
    core = lax.rem(vir, 2)
    chip = occ * 2 + vir // 2
    side = aux // Z
    block = lax.rem(aux, Z) // BLOCKS
    place = lax.rem(aux, BLOCKS)
    role = lax.rem(side * BLOCKS + place + BLOCKS * core, NEAR)
    owner = role < OWNERS
    own = pl.ds(role * SHARE, SHARE)

    def near(other):
        spot_of = lax.rem(other + BLOCKS * core, NEAR)
        return {"aux": (spot_of // BLOCKS) * Z + block * BLOCKS + lax.rem(spot_of, BLOCKS)}

    def far(d):
        return {"aux": side * Z + lax.rem(block + d, BLOCKS) * BLOCKS + place}

    def mate(d):
        other = lax.rem(spot + d, OCC_WAYS * VIR_WAYS)
        return {"occ": other // VIR_WAYS, "vir": lax.rem(other, VIR_WAYS)}

    peers = [near(lax.rem(role + d, NEAR)) for d in range(1, NEAR)]
    crosses = [far(d) for d in range(1, BLOCKS)]
    mates = [mate(d) for d in range(1, OCC_WAYS * VIR_WAYS)]

    loads = [
        pltpu.make_async_copy(start_hbm, start, in_sem.at[0]),
        pltpu.make_async_copy(occ_hbm, eocc, in_sem.at[1]),
        pltpu.make_async_copy(vir_hbm, evir, in_sem.at[2]),
    ]
    fac_loads = [
        pltpu.make_async_copy(
            fac_hbm.at[:, pl.ds(GROUP * c, GROUP)], fac.at[:, pl.ds(GROUP * c, GROUP)], fac_sem.at[c]
        )
        for c in range(ROWS // GROUP)
    ]
    for load in loads:
        load.start()

    barrier = pltpu.get_barrier_semaphore()

    greeted = crosses + peers + mates
    for index, device in enumerate(greeted):
        pl.semaphore_signal(barrier, inc=1, device_id=device, device_id_type=MESH)
        if index == len(crosses) - 1:
            for load in fac_loads:
                load.start()

    for load in loads:
        load.wait()

    def delta(i):
        return evir[...] - eocc[i]

    def contract(source, waits):
        sums = [None, None]
        for i in range(0, ROWS, 2):
            if waits and i % GROUP == 0:
                fac_loads[i // GROUP].wait()
            left = jnp.concatenate([split(source[i]), split(source[i + 1])], axis=1)
            for s in range(2):
                right = jnp.concatenate([fac[s, i], fac[s, i + 1]], axis=1)
                term = lax.dot_general(
                    left, right, (((1,), (1,)), ((), ())), preferred_element_type=f32
                )
                sums[s] = term if sums[s] is None else sums[s] + term
        return [merge(sums[s])[:, LANES * h:LANES * (h + 1)] for s in range(2) for h in range(2)]

    def wait_bytes(ref, sem):
        pltpu.make_async_copy(ref, ref, sem).wait()

    def sum_group(step, tiles, first):
        for index, value in enumerate(tiles):
            cc[step, core, index] = value
        if first:
            pl.semaphore_wait(barrier, len(greeted))
        send(
            cc.at[step, core], cc.at[step, core], (cc_send.at[step], cc_recv.at[step]),
            {"vir": vir + 1 - 2 * core},
        )
        wait_bytes(cc.at[step, 0], cc_recv.at[step])
        for index in range(len(tiles)):
            cm[step, chip, index] = cc[step, 0, index] + cc[step, 1, index]
        for d in range(1, CHIPS):
            other = lax.rem(chip + d, CHIPS)
            send(
                cm.at[step, chip], cm.at[step, chip], (cm_send.at[step], cm_recv.at[step]),
                {"occ": other // 2, "vir": lax.rem(other, 2) * 2 + core},
            )
        wait_bytes(cm.at[step, pl.ds(0, CHIPS - 1)], cm_recv.at[step])
        out = []
        for index in range(len(tiles)):
            sums = [cm[step, j, index] for j in range(CHIPS)]
            while len(sums) > 1:
                sums = [a + b for a, b in zip(sums[0::2], sums[1::2])]
            out.append(sums[0])
        return out

    def send(source, target, sems, device):
        pltpu.make_async_remote_copy(
            src_ref=source, dst_ref=target, send_sem=sems[0], recv_sem=sems[1],
            device_id=device, device_id_type=MESH,
        ).start()

    def scatter(step):
        for d in range(1, NEAR):
            other = lax.rem(role + d, NEAR)

            @pl.when(other < OWNERS)
            def _():
                send(
                    part.at[step, pl.ds(other * SHARE, SHARE)], rs.at[step, role],
                    (rs_send.at[step], rs_recv.at[step]), peers[d - 1],
                )

        @pl.when(owner)
        def _():
            rs[step, role] = part[step, own]

    def back(step, sums):
        scaled = [
            split(jnp.concatenate([2.0 * sums[0], 2.0 * sums[1]], axis=1)),
            split(jnp.concatenate([-sums[2], -sums[3]], axis=1)),
        ]
        for i in range(0, ROWS, 2):
            both = None
            for s in range(2):
                right = jnp.concatenate([fac[s, i], fac[s, i + 1]], axis=1)
                term = lax.dot_general(
                    scaled[s], right, (((1,), (0,)), ((), ())), preferred_element_type=f32
                )
                both = term if both is None else both + term
            both = merge(both)
            part[step, i] = both[:, :LANES]
            part[step, i + 1] = both[:, LANES:]
        scatter(step)

    def spread(step, lower, turned, extra):
        @pl.when(owner)
        def _():
            wait_bytes(rs.at[step, pl.ds(0, NEAR - 1)], rs_recv.at[step])
            sums = [rs[step, j] for j in range(NEAR)]
            while len(sums) > 1:
                sums = [a + b for a, b in zip(sums[0::2], sums[1::2])]
            cx[step, block] = sums[0]
            for d in range(1, BLOCKS):
                send(
                    cx.at[step, block], cx.at[step, block],
                    (cx_send.at[step], cx_recv.at[step]), crosses[d - 1],
                )
            wait_bytes(cx.at[step, pl.ds(0, BLOCKS - 1)], cx_recv.at[step])
            total = (cx[step, 0] + cx[step, 1]) + (cx[step, 2] + cx[step, 3])
            for k in range(SHARE - 1):
                ag[step, role * SHARE + k] = apply(lower, total[k], NV)
            last = role * SHARE + SHARE - 1

            @pl.when(role < OWNERS - 1)
            def _():
                ag[step, last] = apply(lower, total[SHARE - 1], NV)

            @pl.when(role == OWNERS - 1)
            def _():
                half = apply(lower, (total[SHARE - 1] + extra) * (1.0 / PAIRS), NV)
                whole = apply(half, turned)
                ag[step, last] = jnp.where(lane < NV, whole, half)

            for device in peers:
                send(
                    ag.at[step, own], ag.at[step, own],
                    (ag_send.at[step], ag_recv.at[step]), device,
                )
            wait_bytes(ag.at[step, pl.ds(0, TILES - SHARE)], ag_recv.at[step])

        @pl.when(jnp.logical_not(owner))
        def _():
            wait_bytes(ag.at[step], ag_recv.at[step])

    def small(left, right):
        return lax.dot_general(
            left, right, (((1,), (1,)), ((), ())),
            precision=lax.Precision.HIGHEST, preferred_element_type=f32,
        )

    def wide(value):
        return jnp.concatenate(
            [value, jnp.zeros((value.shape[0], LANES - value.shape[1]), f32)], axis=1
        )

    row, lane = iotas()
    weights = [2.0, 2.0, -1.0, -1.0]

    def turn(lower):
        return wide(small(jnp.where(lane == row, 1.0, 0.0)[:, :NV], lower[:, NV:2 * NV]))

    vecs = [start[i] for i in range(ROWS)]
    shifted = [vecs[i] * delta(i) for i in range(ROWS)]
    grams = columns(products(vecs, vecs) + products(vecs, shifted))
    sums = contract(vecs, True)
    *sums, grams = sum_group(0, sums + [grams], True)
    part[0, ROWS] = columns(products([w * v for w, v in zip(weights, sums)], sums))
    back(0, sums)
    lower = factor(grams * (1.0 / PAIRS))
    for index in range(4):
        xhat[index] = apply(lower, sums[index], NV)
    for i in range(ROWS):
        q1[i] = apply(lower, start[i], NV)
    extra = jnp.where(lane < NV, pltpu.roll(grams, LANES - NV, 1), 0.0)
    spread(0, lower, turn(lower), extra)
    proj = ag[0, ROWS]
    coef_ref[0] = proj
    for i in range(ROWS):
        r1[i] = ag[0, i] + delta(i) * q1[i] - apply(proj, q1[i])

    vecs = [r1[i] for i in range(ROWS)]
    moved = [delta(i) * q1[i] for i in range(ROWS)]
    shifted = [vecs[i] * delta(i) for i in range(ROWS)]
    grams = columns(products(vecs, vecs) + products(vecs, shifted) + products(vecs, moved))
    sums = contract(vecs, False)
    *sums, grams = sum_group(1, sums + [grams], False)
    scaled = [w * v for w, v in zip(weights, sums)]
    part[1, ROWS] = columns(products(scaled, sums) + products(scaled, [xhat[k] for k in range(4)]))
    back(1, sums)
    lower = factor(grams * (1.0 / PAIRS))
    coef_ref[1] = jnp.where(lane >= row, lower, 0.0)
    for i in range(ROWS):
        q2[i] = apply(lower, r1[i], NV)
    extra = jnp.where(lane < 2 * NV, pltpu.roll(grams, LANES - NV, 1), 0.0)
    spread(1, lower, turn(lower), extra)
    proj = ag[1, ROWS]
    coef_ref[2] = proj
    for i in range(ROWS):
        resid_ref[i] = ag[1, i] + delta(i) * q2[i] - apply(proj, q2[i]) - apply(proj, q1[i], NV)

    vecs = [resid_ref[i] for i in range(ROWS)]
    gm[spot] = columns(products(vecs, vecs))

    for device in mates:
        send(gm.at[spot], gm.at[spot], (g_send, g_recv), device)
    wait_bytes(gm.at[pl.ds(0, OCC_WAYS * VIR_WAYS - 1)], g_recv)
    sums = [gm[j] for j in range(OCC_WAYS * VIR_WAYS)]
    while len(sums) > 1:
        sums = [a + b for a, b in zip(sums[0::2], sums[1::2])]
    coef_ref[3] = sums[0] * (1.0 / PAIRS)

    for step in range(2):
        wait_bytes(cc.at[step, 0], cc_send.at[step])
        wait_bytes(cm.at[step, pl.ds(0, CHIPS - 1)], cm_send.at[step])

        @pl.when(owner)
        def _():
            wait_bytes(part.at[step, pl.ds(0, TILES - SHARE)], rs_send.at[step])
            wait_bytes(cx.at[step, pl.ds(0, BLOCKS - 1)], cx_send.at[step])
            wait_bytes(rs.at[step, pl.ds(0, NEAR - 1)], ag_send.at[step])

        @pl.when(jnp.logical_not(owner))
        def _():
            wait_bytes(part.at[step], rs_send.at[step])

    wait_bytes(gm.at[pl.ds(0, OCC_WAYS * VIR_WAYS - 1)], g_send)


def finish(small_ref, resid_ref, coef_ref, next_ref):
    row, lane = iotas()
    lower = factor(small_ref[3])
    for k in range(3):
        coef_ref[k] = small_ref[k][:, :NV]
    coef_ref[3] = jnp.where(lane >= row, lower, 0.0)[:, :NV]
    for i in range(ROWS):
        next_ref[i] = apply(lower, resid_ref[i], NV)


def on_device(start_block, factors, eps_occ, eps_vir):
    tile_shape = (NV, LANES)
    dma = pltpu.SemaphoreType.DMA
    anywhere = pl.BlockSpec(memory_space=pltpu.MemorySpace.HBM)
    vmem = pl.BlockSpec(memory_space=pltpu.MemorySpace.VMEM)
    small, resid = pl.pallas_call(
        kernel,
        out_shape=(
            pltpu.VMEM((4,) + tile_shape, f32),
            pltpu.VMEM((ROWS,) + tile_shape, f32),
        ),
        in_specs=[anywhere] * 4,
        out_specs=(vmem, vmem),
        scratch_shapes=[
            pltpu.VMEM((ROWS,) + tile_shape, f32),
            pltpu.VMEM((2, ROWS, DEPTH, LANES), bf16),
            pltpu.SMEM((ROWS,), f32),
            pltpu.VMEM((1, LANES), f32),
            pltpu.VMEM((ROWS,) + tile_shape, f32),
            pltpu.VMEM((ROWS,) + tile_shape, f32),
            pltpu.VMEM((ROWS,) + tile_shape, f32),
            pltpu.VMEM((4,) + tile_shape, f32),
            pltpu.VMEM((2, 2, 5) + tile_shape, f32),
            pltpu.VMEM((2, CHIPS, 5) + tile_shape, f32),
            pltpu.VMEM((2, TILES) + tile_shape, f32),
            pltpu.VMEM((2, NEAR, SHARE) + tile_shape, f32),
            pltpu.VMEM((2, BLOCKS, SHARE) + tile_shape, f32),
            pltpu.VMEM((2, TILES) + tile_shape, f32),
            pltpu.VMEM((OCC_WAYS * VIR_WAYS,) + tile_shape, f32),
            dma((3,)), dma((ROWS // GROUP,)),
            dma((2,)), dma((2,)), dma((2,)), dma((2,)),
            dma((2,)), dma((2,)), dma((2,)), dma((2,)), dma((2,)), dma((2,)),
            dma, dma,
        ],
        compiler_params=pltpu.CompilerParams(
            collective_id=0, has_side_effects=True, vmem_limit_bytes=60 * 1024 * 1024
        ),
        cost_estimate=pl.CostEstimate(flops=200_000_000, bytes_accessed=3_000_000, transcendentals=0),
    )(
        start_block.transpose(1, 0, 2),
        factors.transpose(0, 2, 1, 3),
        eps_occ,
        eps_vir.reshape(1, LANES),
    )
    coefs, block = pl.pallas_call(
        finish,
        out_shape=(
            jax.ShapeDtypeStruct((4, NV, NV), f32),
            jax.ShapeDtypeStruct((ROWS,) + tile_shape, f32),
        ),
        in_specs=[vmem] * 2,
        out_specs=(vmem, vmem),
        compiler_params=pltpu.CompilerParams(vmem_limit_bytes=4 * 1024 * 1024),
        cost_estimate=pl.CostEstimate(flops=400_000, bytes_accessed=200_000, transcendentals=0),
    )(small, resid)
    return coefs, block.transpose(1, 0, 2)


def solution(mesh):
    placed = (P(None, "occ", "vir"), P(None, "aux", "occ", "vir"), P("occ"), P("vir"))
    return jax.shard_map(
        on_device,
        mesh=mesh,
        in_specs=placed,
        out_specs=(P(), P(None, "occ", "vir")),
        check_vma=False,
    )
```

```python
import jax
import jax.numpy as jnp
from jax import lax
from jax.experimental import pallas as pl
from jax.experimental.pallas import tpu as pltpu
from jax.sharding import PartitionSpec as P

OCC_WAYS, VIR_WAYS = 4, 4
NV, ROWS, LANES, DEPTH = 8, 20, 128, 256
PAIRS = 40960
TILES = ROWS + 1
NEAR, BLOCKS, Z, SHARE = 8, 4, 16, 3
OWNERS = TILES // SHARE
SHIFT = 2
CHIPS = 8
GROUP = 4
MESH = pl.DeviceIdType.MESH
f32, bf16 = jnp.float32, jnp.bfloat16


def split(value):
    high = value.astype(bf16)
    low = (value - high.astype(f32)).astype(bf16)
    return jnp.concatenate([high, low], axis=0)


def merge(value):
    return value[:NV] + value[NV:]


def apply(matrix, value, first=0):
    total = matrix[:, first:first + 1] * value[0:1, :]
    for m in range(1, NV):
        total = total + matrix[:, first + m:first + m + 1] * value[m:m + 1, :]
    return total


def iotas():
    return (
        lax.broadcasted_iota(jnp.int32, (NV, LANES), 0),
        lax.broadcasted_iota(jnp.int32, (NV, LANES), 1),
    )


def factor(gram):
    row, lane = iotas()
    work = jnp.where(lane < NV, gram, jnp.where(lane == row + NV, 1.0, 0.0))
    scale = jnp.ones((NV, 1), f32)
    rows1 = lax.broadcasted_iota(jnp.int32, (NV, 1), 0)
    for k in range(NV):
        pivot = work[k:k + 1, k:k + 1]
        scale = jnp.where(rows1 == k, pivot, scale)
        if k < NV - 1:
            ratio = jnp.where(rows1 > k, work[:, k:k + 1] / pivot, 0.0)
            work = work - ratio * work[k:k + 1, :]
    return work * (1.0 / jnp.sqrt(scale))


def columns(sums):
    _, lane = iotas()
    out = jnp.zeros((NV, LANES), f32)
    for m, value in enumerate(sums):
        out = jnp.where(lane == m, jnp.sum(value, axis=1, keepdims=True), out)
    return out


def products(lefts, rights):
    sums = []
    for m in range(NV):
        total = lefts[0] * rights[0][m:m + 1, :]
        for left, right in zip(lefts[1:], rights[1:]):
            total = total + left * right[m:m + 1, :]
        sums.append(total)
    return sums


def kernel(
    start_hbm, fac_hbm, occ_hbm, vir_hbm,
    coef_ref, resid_ref,
    start, fac, eocc, evir, q1, q2, r1, xhat,
    cc, cm, part, rs, cx, ag, gm,
    in_sem, fac_sem, cc_send, cc_recv, cm_send, cm_recv,
    rs_send, rs_recv, cx_send, cx_recv, ag_send, ag_recv, g_send, g_recv,
):
    aux = lax.axis_index("aux")
    occ = lax.axis_index("occ")
    vir = lax.axis_index("vir")
    spot = occ * VIR_WAYS + vir
    core = lax.rem(vir, 2)
    chip = occ * 2 + vir // 2
    side = aux // Z
    along = lax.rem(lax.rem(aux, Z) + SHIFT * core, Z)
    block = along // BLOCKS
    place = lax.rem(along, BLOCKS)
    role = lax.rem(side * BLOCKS + place + BLOCKS * core, NEAR)
    owner = role < OWNERS
    own = pl.ds(role * SHARE, SHARE)

    def at(side_of, block_of, place_of):
        z = lax.rem(block_of * BLOCKS + place_of + Z - SHIFT * core, Z)
        return {"aux": side_of * Z + z}

    def near(other):
        spot_of = lax.rem(other + BLOCKS * core, NEAR)
        return at(spot_of // BLOCKS, block, lax.rem(spot_of, BLOCKS))

    def far(d):
        return at(side, lax.rem(block + d, BLOCKS), place)

    def mate(d):
        other = lax.rem(spot + d, OCC_WAYS * VIR_WAYS)
        return {"occ": other // VIR_WAYS, "vir": lax.rem(other, VIR_WAYS)}

    peers = [near(lax.rem(role + d, NEAR)) for d in range(1, NEAR)]
    crosses = [far(d) for d in range(1, BLOCKS)]
    mates = [mate(d) for d in range(1, OCC_WAYS * VIR_WAYS)]

    loads = [
        pltpu.make_async_copy(start_hbm, start, in_sem.at[0]),
        pltpu.make_async_copy(occ_hbm, eocc, in_sem.at[1]),
        pltpu.make_async_copy(vir_hbm, evir, in_sem.at[2]),
    ]
    fac_loads = [
        pltpu.make_async_copy(
            fac_hbm.at[:, pl.ds(GROUP * c, GROUP)], fac.at[:, pl.ds(GROUP * c, GROUP)], fac_sem.at[c]
        )
        for c in range(ROWS // GROUP)
    ]
    for load in loads:
        load.start()

    barrier = pltpu.get_barrier_semaphore()

    greeted = crosses + peers + mates
    for index, device in enumerate(greeted):
        pl.semaphore_signal(barrier, inc=1, device_id=device, device_id_type=MESH)
        if index == len(crosses) - 1:
            for load in fac_loads:
                load.start()

    for load in loads:
        load.wait()

    def delta(i):
        return evir[...] - eocc[i]

    def contract(source, waits):
        sums = [None, None]
        for i in range(0, ROWS, 2):
            if waits and i % GROUP == 0:
                fac_loads[i // GROUP].wait()
            left = jnp.concatenate([split(source[i]), split(source[i + 1])], axis=1)
            for s in range(2):
                right = jnp.concatenate([fac[s, i], fac[s, i + 1]], axis=1)
                term = lax.dot_general(
                    left, right, (((1,), (1,)), ((), ())), preferred_element_type=f32
                )
                sums[s] = term if sums[s] is None else sums[s] + term
        return [merge(sums[s])[:, LANES * h:LANES * (h + 1)] for s in range(2) for h in range(2)]

    def wait_bytes(ref, sem):
        pltpu.make_async_copy(ref, ref, sem).wait()

    def sum_group(step, tiles, first):
        for index, value in enumerate(tiles):
            cc[step, core, index] = value
        if first:
            pl.semaphore_wait(barrier, len(greeted))
        send(
            cc.at[step, core], cc.at[step, core], (cc_send.at[step], cc_recv.at[step]),
            {"vir": vir + 1 - 2 * core},
        )
        wait_bytes(cc.at[step, 0], cc_recv.at[step])
        for index in range(len(tiles)):
            cm[step, chip, index] = cc[step, 0, index] + cc[step, 1, index]
        for d in range(1, CHIPS):
            other = lax.rem(chip + d, CHIPS)
            send(
                cm.at[step, chip], cm.at[step, chip], (cm_send.at[step], cm_recv.at[step]),
                {"occ": other // 2, "vir": lax.rem(other, 2) * 2 + core},
            )
        wait_bytes(cm.at[step, pl.ds(0, CHIPS - 1)], cm_recv.at[step])
        out = []
        for index in range(len(tiles)):
            sums = [cm[step, j, index] for j in range(CHIPS)]
            while len(sums) > 1:
                sums = [a + b for a, b in zip(sums[0::2], sums[1::2])]
            out.append(sums[0])
        return out

    def send(source, target, sems, device):
        pltpu.make_async_remote_copy(
            src_ref=source, dst_ref=target, send_sem=sems[0], recv_sem=sems[1],
            device_id=device, device_id_type=MESH,
        ).start()

    def scatter(step):
        for d in range(1, NEAR):
            other = lax.rem(role + d, NEAR)

            @pl.when(other < OWNERS)
            def _():
                send(
                    part.at[step, pl.ds(other * SHARE, SHARE)], rs.at[step, role],
                    (rs_send.at[step], rs_recv.at[step]), peers[d - 1],
                )

        @pl.when(owner)
        def _():
            rs[step, role] = part[step, own]

    def back(step, sums):
        scaled = [
            split(jnp.concatenate([2.0 * sums[0], 2.0 * sums[1]], axis=1)),
            split(jnp.concatenate([-sums[2], -sums[3]], axis=1)),
        ]
        for i in range(0, ROWS, 2):
            both = None
            for s in range(2):
                right = jnp.concatenate([fac[s, i], fac[s, i + 1]], axis=1)
                term = lax.dot_general(
                    scaled[s], right, (((1,), (0,)), ((), ())), preferred_element_type=f32
                )
                both = term if both is None else both + term
            both = merge(both)
            part[step, i] = both[:, :LANES]
            part[step, i + 1] = both[:, LANES:]
        scatter(step)

    def spread(step, lower, turned, extra):
        @pl.when(owner)
        def _():
            wait_bytes(rs.at[step, pl.ds(0, NEAR - 1)], rs_recv.at[step])
            sums = [rs[step, j] for j in range(NEAR)]
            while len(sums) > 1:
                sums = [a + b for a, b in zip(sums[0::2], sums[1::2])]
            cx[step, block] = sums[0]
            for d in range(1, BLOCKS):
                send(
                    cx.at[step, block], cx.at[step, block],
                    (cx_send.at[step], cx_recv.at[step]), crosses[d - 1],
                )
            wait_bytes(cx.at[step, pl.ds(0, BLOCKS - 1)], cx_recv.at[step])
            total = (cx[step, 0] + cx[step, 1]) + (cx[step, 2] + cx[step, 3])
            for k in range(SHARE - 1):
                ag[step, role * SHARE + k] = apply(lower, total[k], NV)
            last = role * SHARE + SHARE - 1

            @pl.when(role < OWNERS - 1)
            def _():
                ag[step, last] = apply(lower, total[SHARE - 1], NV)

            @pl.when(role == OWNERS - 1)
            def _():
                half = apply(lower, (total[SHARE - 1] + extra) * (1.0 / PAIRS), NV)
                whole = apply(half, turned)
                ag[step, last] = jnp.where(lane < NV, whole, half)

            for device in peers:
                send(
                    ag.at[step, own], ag.at[step, own],
                    (ag_send.at[step], ag_recv.at[step]), device,
                )
            wait_bytes(ag.at[step, pl.ds(0, TILES - SHARE)], ag_recv.at[step])

        @pl.when(jnp.logical_not(owner))
        def _():
            wait_bytes(ag.at[step], ag_recv.at[step])

    def small(left, right):
        return lax.dot_general(
            left, right, (((1,), (1,)), ((), ())),
            precision=lax.Precision.HIGHEST, preferred_element_type=f32,
        )

    def wide(value):
        return jnp.concatenate(
            [value, jnp.zeros((value.shape[0], LANES - value.shape[1]), f32)], axis=1
        )

    row, lane = iotas()
    weights = [2.0, 2.0, -1.0, -1.0]

    def turn(lower):
        return wide(small(jnp.where(lane == row, 1.0, 0.0)[:, :NV], lower[:, NV:2 * NV]))

    vecs = [start[i] for i in range(ROWS)]
    shifted = [vecs[i] * delta(i) for i in range(ROWS)]
    grams = columns(products(vecs, vecs) + products(vecs, shifted))
    sums = contract(vecs, True)
    *sums, grams = sum_group(0, sums + [grams], True)
    part[0, ROWS] = columns(products([w * v for w, v in zip(weights, sums)], sums))
    back(0, sums)
    lower = factor(grams * (1.0 / PAIRS))
    for index in range(4):
        xhat[index] = apply(lower, sums[index], NV)
    for i in range(ROWS):
        q1[i] = apply(lower, start[i], NV)
    extra = jnp.where(lane < NV, pltpu.roll(grams, LANES - NV, 1), 0.0)
    spread(0, lower, turn(lower), extra)
    proj = ag[0, ROWS]
    proj1 = proj
    for i in range(ROWS):
        r1[i] = ag[0, i] + delta(i) * q1[i] - apply(proj, q1[i])

    vecs = [r1[i] for i in range(ROWS)]
    moved = [delta(i) * q1[i] for i in range(ROWS)]
    shifted = [vecs[i] * delta(i) for i in range(ROWS)]
    grams = columns(products(vecs, vecs) + products(vecs, shifted) + products(vecs, moved))
    sums = contract(vecs, False)
    *sums, grams = sum_group(1, sums + [grams], False)
    scaled = [w * v for w, v in zip(weights, sums)]
    part[1, ROWS] = columns(products(scaled, sums) + products(scaled, [xhat[k] for k in range(4)]))
    back(1, sums)
    lower = factor(grams * (1.0 / PAIRS))
    coef_ref[1] = jnp.where(lane >= row, lower, 0.0)
    for i in range(ROWS):
        q2[i] = apply(lower, r1[i], NV)
    extra = jnp.where(lane < 2 * NV, pltpu.roll(grams, LANES - NV, 1), 0.0)
    spread(1, lower, turn(lower), extra)
    proj = ag[1, ROWS]
    for i in range(ROWS):
        resid_ref[i] = ag[1, i] + delta(i) * q2[i] - apply(proj, q2[i]) - apply(proj, q1[i], NV)

    vecs = [resid_ref[i] for i in range(ROWS)]
    grams = columns(products(vecs, vecs))
    grams = jnp.where(jnp.logical_and(lane >= NV, lane < 2 * NV), pltpu.roll(proj1, NV, 1), grams)
    grams = jnp.where(
        jnp.logical_and(lane >= 2 * NV, lane < 3 * NV), pltpu.roll(proj, 2 * NV, 1), grams
    )
    gm[spot] = grams

    for device in mates:
        send(gm.at[spot], gm.at[spot], (g_send, g_recv), device)
    wait_bytes(gm.at[pl.ds(0, OCC_WAYS * VIR_WAYS - 1)], g_recv)
    sums = [gm[j] for j in range(OCC_WAYS * VIR_WAYS)]
    while len(sums) > 1:
        sums = [a + b for a, b in zip(sums[0::2], sums[1::2])]
    coef_ref[3] = sums[0] * (1.0 / PAIRS)
    coef_ref[0] = pltpu.roll(gm[0], LANES - NV, 1)
    coef_ref[2] = pltpu.roll(gm[0], LANES - 2 * NV, 1)

    for step in range(2):
        wait_bytes(cc.at[step, 0], cc_send.at[step])
        wait_bytes(cm.at[step, pl.ds(0, CHIPS - 1)], cm_send.at[step])

        @pl.when(owner)
        def _():
            wait_bytes(part.at[step, pl.ds(0, TILES - SHARE)], rs_send.at[step])
            wait_bytes(cx.at[step, pl.ds(0, BLOCKS - 1)], cx_send.at[step])
            wait_bytes(rs.at[step, pl.ds(0, NEAR - 1)], ag_send.at[step])

        @pl.when(jnp.logical_not(owner))
        def _():
            wait_bytes(part.at[step], rs_send.at[step])

    wait_bytes(gm.at[pl.ds(0, OCC_WAYS * VIR_WAYS - 1)], g_send)


def finish(small_ref, resid_ref, coef_ref, next_ref):
    row, lane = iotas()
    lower = factor(small_ref[3])
    for k in range(3):
        coef_ref[k] = small_ref[k][:, :NV]
    coef_ref[3] = jnp.where(lane >= row, lower, 0.0)[:, :NV]
    for i in range(ROWS):
        next_ref[i] = apply(lower, resid_ref[i], NV)


def on_device(start_block, factors, eps_occ, eps_vir):
    tile_shape = (NV, LANES)
    dma = pltpu.SemaphoreType.DMA
    anywhere = pl.BlockSpec(memory_space=pltpu.MemorySpace.HBM)
    vmem = pl.BlockSpec(memory_space=pltpu.MemorySpace.VMEM)
    small, resid = pl.pallas_call(
        kernel,
        out_shape=(
            pltpu.VMEM((4,) + tile_shape, f32),
            pltpu.VMEM((ROWS,) + tile_shape, f32),
        ),
        in_specs=[anywhere] * 4,
        out_specs=(vmem, vmem),
        scratch_shapes=[
            pltpu.VMEM((ROWS,) + tile_shape, f32),
            pltpu.VMEM((2, ROWS, DEPTH, LANES), bf16),
            pltpu.SMEM((ROWS,), f32),
            pltpu.VMEM((1, LANES), f32),
            pltpu.VMEM((ROWS,) + tile_shape, f32),
            pltpu.VMEM((ROWS,) + tile_shape, f32),
            pltpu.VMEM((ROWS,) + tile_shape, f32),
            pltpu.VMEM((4,) + tile_shape, f32),
            pltpu.VMEM((2, 2, 5) + tile_shape, f32),
            pltpu.VMEM((2, CHIPS, 5) + tile_shape, f32),
            pltpu.VMEM((2, TILES) + tile_shape, f32),
            pltpu.VMEM((2, NEAR, SHARE) + tile_shape, f32),
            pltpu.VMEM((2, BLOCKS, SHARE) + tile_shape, f32),
            pltpu.VMEM((2, TILES) + tile_shape, f32),
            pltpu.VMEM((OCC_WAYS * VIR_WAYS,) + tile_shape, f32),
            dma((3,)), dma((ROWS // GROUP,)),
            dma((2,)), dma((2,)), dma((2,)), dma((2,)),
            dma((2,)), dma((2,)), dma((2,)), dma((2,)), dma((2,)), dma((2,)),
            dma, dma,
        ],
        compiler_params=pltpu.CompilerParams(
            collective_id=0, has_side_effects=True, vmem_limit_bytes=60 * 1024 * 1024
        ),
        cost_estimate=pl.CostEstimate(flops=200_000_000, bytes_accessed=3_000_000, transcendentals=0),
    )(
        start_block.transpose(1, 0, 2),
        factors.transpose(0, 2, 1, 3),
        eps_occ,
        eps_vir.reshape(1, LANES),
    )
    coefs, block = pl.pallas_call(
        finish,
        out_shape=(
            jax.ShapeDtypeStruct((4, NV, NV), f32),
            jax.ShapeDtypeStruct((ROWS,) + tile_shape, f32),
        ),
        in_specs=[vmem] * 2,
        out_specs=(vmem, vmem),
        compiler_params=pltpu.CompilerParams(vmem_limit_bytes=4 * 1024 * 1024),
        cost_estimate=pl.CostEstimate(flops=400_000, bytes_accessed=200_000, transcendentals=0),
    )(small, resid)
    return coefs, block.transpose(1, 0, 2)


def solution(mesh):
    placed = (P(None, "occ", "vir"), P(None, "aux", "occ", "vir"), P("occ"), P("vir"))
    return jax.shard_map(
        on_device,
        mesh=mesh,
        in_specs=placed,
        out_specs=(P(), P(None, "occ", "vir")),
        check_vma=False,
    )
```

```python
import jax
import jax.numpy as jnp
from jax import lax
from jax.experimental import pallas as pl
from jax.experimental.pallas import tpu as pltpu
from jax.sharding import PartitionSpec as P

OCC_WAYS, VIR_WAYS = 4, 4
NV, ROWS, LANES, DEPTH = 8, 20, 128, 256
PAIRS = 40960
TILES = ROWS + 1
NEAR, BLOCKS, Z, SHARE = 8, 4, 16, 3
OWNERS = TILES // SHARE
CHIPS = 8
GROUP = 4
MESH = pl.DeviceIdType.MESH
f32, bf16 = jnp.float32, jnp.bfloat16


def split(value):
    high = value.astype(bf16)
    low = (value - high.astype(f32)).astype(bf16)
    return jnp.concatenate([high, low], axis=0)


def merge(value):
    return value[:NV] + value[NV:]


def apply(matrix, value, first=0):
    total = matrix[:, first:first + 1] * value[0:1, :]
    for m in range(1, NV):
        total = total + matrix[:, first + m:first + m + 1] * value[m:m + 1, :]
    return total


def iotas():
    return (
        lax.broadcasted_iota(jnp.int32, (NV, LANES), 0),
        lax.broadcasted_iota(jnp.int32, (NV, LANES), 1),
    )


def factor(gram):
    row, lane = iotas()
    work = jnp.where(lane < NV, gram, jnp.where(lane == row + NV, 1.0, 0.0))
    scale = jnp.ones((NV, 1), f32)
    rows1 = lax.broadcasted_iota(jnp.int32, (NV, 1), 0)
    for k in range(NV):
        pivot = work[k:k + 1, k:k + 1]
        scale = jnp.where(rows1 == k, pivot, scale)
        if k < NV - 1:
            ratio = jnp.where(rows1 > k, work[:, k:k + 1] / pivot, 0.0)
            work = work - ratio * work[k:k + 1, :]
    return work * (1.0 / jnp.sqrt(scale))


def columns(sums):
    _, lane = iotas()
    out = jnp.zeros((NV, LANES), f32)
    for m, value in enumerate(sums):
        out = jnp.where(lane == m, jnp.sum(value, axis=1, keepdims=True), out)
    return out


def products(lefts, rights):
    sums = []
    for m in range(NV):
        total = lefts[0] * rights[0][m:m + 1, :]
        for left, right in zip(lefts[1:], rights[1:]):
            total = total + left * right[m:m + 1, :]
        sums.append(total)
    return sums


def kernel(
    start_hbm, fac_hbm, occ_hbm, vir_hbm,
    coef_ref, resid_ref,
    start, fac, eocc, evir, q1, q2, r1, xhat,
    cc, cm, part, rs, cx, ag, gm,
    in_sem, fac_sem, cc_send, cc_recv, cm_send, cm_recv,
    rs_send, rs_recv, cx_send, cx_recv, ag_send, ag_recv, g_send, g_recv,
):
    aux = lax.axis_index("aux")
    occ = lax.axis_index("occ")
    vir = lax.axis_index("vir")
    spot = occ * VIR_WAYS + vir
    core = lax.rem(vir, 2)
    chip = occ * 2 + vir // 2
    side = aux // Z
    block = lax.rem(aux, Z) // BLOCKS
    place = lax.rem(aux, BLOCKS)
    role = lax.rem(side * BLOCKS + place + BLOCKS * core, NEAR)
    owner = role < OWNERS
    own = pl.ds(role * SHARE, SHARE)

    def near(other):
        spot_of = lax.rem(other + BLOCKS * core, NEAR)
        return {"aux": (spot_of // BLOCKS) * Z + block * BLOCKS + lax.rem(spot_of, BLOCKS)}

    def far(d):
        return {"aux": side * Z + lax.rem(block + d, BLOCKS) * BLOCKS + place}

    def mate(d):
        other = lax.rem(spot + d, OCC_WAYS * VIR_WAYS)
        return {"occ": other // VIR_WAYS, "vir": lax.rem(other, VIR_WAYS)}

    peers = [near(lax.rem(role + d, NEAR)) for d in range(1, NEAR)]
    crosses = [far(d) for d in range(1, BLOCKS)]
    mates = [mate(d) for d in range(1, OCC_WAYS * VIR_WAYS)]

    loads = [
        pltpu.make_async_copy(start_hbm, start, in_sem.at[0]),
        pltpu.make_async_copy(occ_hbm, eocc, in_sem.at[1]),
        pltpu.make_async_copy(vir_hbm, evir, in_sem.at[2]),
    ]
    fac_loads = [
        pltpu.make_async_copy(
            fac_hbm.at[:, pl.ds(GROUP * c, GROUP)], fac.at[:, pl.ds(GROUP * c, GROUP)], fac_sem.at[c]
        )
        for c in range(ROWS // GROUP)
    ]
    for load in loads:
        load.start()

    barrier = pltpu.get_barrier_semaphore()

    greeted = crosses + peers + mates
    for index, device in enumerate(greeted):
        pl.semaphore_signal(barrier, inc=1, device_id=device, device_id_type=MESH)
        if index == len(crosses) - 1:
            for load in fac_loads:
                load.start()

    for load in loads:
        load.wait()

    def delta(i):
        return evir[...] - eocc[i]

    def contract(source, waits):
        sums = [None, None]
        for i in range(0, ROWS, 2):
            if waits and i % GROUP == 0:
                fac_loads[i // GROUP].wait()
            left = jnp.concatenate([split(source[i]), split(source[i + 1])], axis=1)
            for s in range(2):
                right = jnp.concatenate([fac[s, i], fac[s, i + 1]], axis=1)
                term = lax.dot_general(
                    left, right, (((1,), (1,)), ((), ())), preferred_element_type=f32
                )
                sums[s] = term if sums[s] is None else sums[s] + term
        return [merge(sums[s])[:, LANES * h:LANES * (h + 1)] for s in range(2) for h in range(2)]

    def wait_bytes(ref, sem):
        pltpu.make_async_copy(ref, ref, sem).wait()

    def sum_group(step, tiles, first, small_products):
        for index, value in enumerate(tiles):
            cc[step, core, index] = value
        if first:
            pl.semaphore_wait(barrier, len(greeted))
        send(
            cc.at[step, core], cc.at[step, core], (cc_send.at[step], cc_recv.at[step]),
            {"vir": vir + 1 - 2 * core},
        )
        hand_out(step, small_products())
        wait_bytes(cc.at[step, 0], cc_recv.at[step])
        for index in range(len(tiles)):
            cm[step, chip, index] = cc[step, 0, index] + cc[step, 1, index]
        for d in range(1, CHIPS):
            other = lax.rem(chip + d, CHIPS)
            send(
                cm.at[step, chip], cm.at[step, chip], (cm_send.at[step], cm_recv.at[step]),
                {"occ": other // 2, "vir": lax.rem(other, 2) * 2 + core},
            )
        wait_bytes(cm.at[step, pl.ds(0, CHIPS - 1)], cm_recv.at[step])
        out = []
        for index in range(len(tiles)):
            sums = [cm[step, j, index] for j in range(CHIPS)]
            while len(sums) > 1:
                sums = [a + b for a, b in zip(sums[0::2], sums[1::2])]
            out.append(sums[0])
        return out

    def hand_out(k, value):
        gm[k, spot] = value
        for device in mates:
            send(gm.at[k, spot], gm.at[k, spot], (g_send.at[k], g_recv.at[k]), device)

    def gather(k):
        wait_bytes(gm.at[k, pl.ds(0, len(mates))], g_recv.at[k])
        sums = [gm[k, j] for j in range(OCC_WAYS * VIR_WAYS)]
        while len(sums) > 1:
            sums = [a + b for a, b in zip(sums[0::2], sums[1::2])]
        return sums[0]

    def send(source, target, sems, device):
        pltpu.make_async_remote_copy(
            src_ref=source, dst_ref=target, send_sem=sems[0], recv_sem=sems[1],
            device_id=device, device_id_type=MESH,
        ).start()

    def scatter(step):
        for d in range(1, NEAR):
            other = lax.rem(role + d, NEAR)

            @pl.when(other < OWNERS)
            def _():
                send(
                    part.at[step, pl.ds(other * SHARE, SHARE)], rs.at[step, role],
                    (rs_send.at[step], rs_recv.at[step]), peers[d - 1],
                )

        @pl.when(owner)
        def _():
            rs[step, role] = part[step, own]

    def back(step, sums):
        scaled = [
            split(jnp.concatenate([2.0 * sums[0], 2.0 * sums[1]], axis=1)),
            split(jnp.concatenate([-sums[2], -sums[3]], axis=1)),
        ]
        for i in range(0, ROWS, 2):
            both = None
            for s in range(2):
                right = jnp.concatenate([fac[s, i], fac[s, i + 1]], axis=1)
                term = lax.dot_general(
                    scaled[s], right, (((1,), (0,)), ((), ())), preferred_element_type=f32
                )
                both = term if both is None else both + term
            both = merge(both)
            part[step, i] = both[:, :LANES]
            part[step, i + 1] = both[:, LANES:]
        scatter(step)

    def spread(step, lower, turned, extra):
        @pl.when(owner)
        def _():
            wait_bytes(rs.at[step, pl.ds(0, NEAR - 1)], rs_recv.at[step])
            sums = [rs[step, j] for j in range(NEAR)]
            while len(sums) > 1:
                sums = [a + b for a, b in zip(sums[0::2], sums[1::2])]
            cx[step, block] = sums[0]
            for d in range(1, BLOCKS):
                send(
                    cx.at[step, block], cx.at[step, block],
                    (cx_send.at[step], cx_recv.at[step]), crosses[d - 1],
                )
            wait_bytes(cx.at[step, pl.ds(0, BLOCKS - 1)], cx_recv.at[step])
            total = (cx[step, 0] + cx[step, 1]) + (cx[step, 2] + cx[step, 3])
            for k in range(SHARE - 1):
                ag[step, role * SHARE + k] = apply(lower, total[k], NV)
            last = role * SHARE + SHARE - 1

            @pl.when(role < OWNERS - 1)
            def _():
                ag[step, last] = apply(lower, total[SHARE - 1], NV)

            @pl.when(role == OWNERS - 1)
            def _():
                half = apply(lower, (total[SHARE - 1] + extra) * (1.0 / PAIRS), NV)
                whole = apply(half, turned)
                ag[step, last] = jnp.where(lane < NV, whole, half)

            for device in peers:
                send(
                    ag.at[step, own], ag.at[step, own],
                    (ag_send.at[step], ag_recv.at[step]), device,
                )
            wait_bytes(ag.at[step, pl.ds(0, TILES - SHARE)], ag_recv.at[step])

        @pl.when(jnp.logical_not(owner))
        def _():
            wait_bytes(ag.at[step], ag_recv.at[step])

    def small(left, right):
        return lax.dot_general(
            left, right, (((1,), (1,)), ((), ())),
            precision=lax.Precision.HIGHEST, preferred_element_type=f32,
        )

    def wide(value):
        return jnp.concatenate(
            [value, jnp.zeros((value.shape[0], LANES - value.shape[1]), f32)], axis=1
        )

    row, lane = iotas()
    weights = [2.0, 2.0, -1.0, -1.0]

    def turn(lower):
        return wide(small(jnp.where(lane == row, 1.0, 0.0)[:, :NV], lower[:, NV:2 * NV]))

    vecs = [start[i] for i in range(ROWS)]
    shifted = [vecs[i] * delta(i) for i in range(ROWS)]
    sums = sum_group(
        0, contract(vecs, True), True, lambda: columns(products(vecs, vecs) + products(vecs, shifted))
    )
    part[0, ROWS] = columns(products([w * v for w, v in zip(weights, sums)], sums))
    back(0, sums)
    grams = gather(0)
    lower = factor(grams * (1.0 / PAIRS))
    for index in range(4):
        xhat[index] = apply(lower, sums[index], NV)
    for i in range(ROWS):
        q1[i] = apply(lower, start[i], NV)
    extra = jnp.where(lane < NV, pltpu.roll(grams, LANES - NV, 1), 0.0)
    spread(0, lower, turn(lower), extra)
    proj = ag[0, ROWS]
    coef_ref[0] = proj
    for i in range(ROWS):
        r1[i] = ag[0, i] + delta(i) * q1[i] - apply(proj, q1[i])

    vecs = [r1[i] for i in range(ROWS)]
    moved = [delta(i) * q1[i] for i in range(ROWS)]
    shifted = [vecs[i] * delta(i) for i in range(ROWS)]
    sums = sum_group(
        1, contract(vecs, False), False,
        lambda: columns(products(vecs, vecs) + products(vecs, shifted) + products(vecs, moved)),
    )
    scaled = [w * v for w, v in zip(weights, sums)]
    part[1, ROWS] = columns(products(scaled, sums) + products(scaled, [xhat[k] for k in range(4)]))
    back(1, sums)
    grams = gather(1)
    lower = factor(grams * (1.0 / PAIRS))
    coef_ref[1] = jnp.where(lane >= row, lower, 0.0)
    for i in range(ROWS):
        q2[i] = apply(lower, r1[i], NV)
    extra = jnp.where(lane < 2 * NV, pltpu.roll(grams, LANES - NV, 1), 0.0)
    spread(1, lower, turn(lower), extra)
    proj = ag[1, ROWS]
    coef_ref[2] = proj
    for i in range(ROWS):
        resid_ref[i] = ag[1, i] + delta(i) * q2[i] - apply(proj, q2[i]) - apply(proj, q1[i], NV)

    vecs = [resid_ref[i] for i in range(ROWS)]
    hand_out(2, columns(products(vecs, vecs)))
    coef_ref[3] = gather(2) * (1.0 / PAIRS)

    for step in range(2):
        wait_bytes(cc.at[step, 0], cc_send.at[step])
        wait_bytes(cm.at[step, pl.ds(0, CHIPS - 1)], cm_send.at[step])

        @pl.when(owner)
        def _():
            wait_bytes(part.at[step, pl.ds(0, TILES - SHARE)], rs_send.at[step])
            wait_bytes(cx.at[step, pl.ds(0, BLOCKS - 1)], cx_send.at[step])
            wait_bytes(rs.at[step, pl.ds(0, NEAR - 1)], ag_send.at[step])

        @pl.when(jnp.logical_not(owner))
        def _():
            wait_bytes(part.at[step], rs_send.at[step])

    for k in range(3):
        wait_bytes(gm.at[k, pl.ds(0, len(mates))], g_send.at[k])


def finish(small_ref, resid_ref, coef_ref, next_ref):
    row, lane = iotas()
    lower = factor(small_ref[3])
    for k in range(3):
        coef_ref[k] = small_ref[k][:, :NV]
    coef_ref[3] = jnp.where(lane >= row, lower, 0.0)[:, :NV]
    for i in range(ROWS):
        next_ref[i] = apply(lower, resid_ref[i], NV)


def on_device(start_block, factors, eps_occ, eps_vir):
    tile_shape = (NV, LANES)
    dma = pltpu.SemaphoreType.DMA
    anywhere = pl.BlockSpec(memory_space=pltpu.MemorySpace.HBM)
    vmem = pl.BlockSpec(memory_space=pltpu.MemorySpace.VMEM)
    small, resid = pl.pallas_call(
        kernel,
        out_shape=(
            pltpu.VMEM((4,) + tile_shape, f32),
            pltpu.VMEM((ROWS,) + tile_shape, f32),
        ),
        in_specs=[anywhere] * 4,
        out_specs=(vmem, vmem),
        scratch_shapes=[
            pltpu.VMEM((ROWS,) + tile_shape, f32),
            pltpu.VMEM((2, ROWS, DEPTH, LANES), bf16),
            pltpu.SMEM((ROWS,), f32),
            pltpu.VMEM((1, LANES), f32),
            pltpu.VMEM((ROWS,) + tile_shape, f32),
            pltpu.VMEM((ROWS,) + tile_shape, f32),
            pltpu.VMEM((ROWS,) + tile_shape, f32),
            pltpu.VMEM((4,) + tile_shape, f32),
            pltpu.VMEM((2, 2, 4) + tile_shape, f32),
            pltpu.VMEM((2, CHIPS, 4) + tile_shape, f32),
            pltpu.VMEM((2, TILES) + tile_shape, f32),
            pltpu.VMEM((2, NEAR, SHARE) + tile_shape, f32),
            pltpu.VMEM((2, BLOCKS, SHARE) + tile_shape, f32),
            pltpu.VMEM((2, TILES) + tile_shape, f32),
            pltpu.VMEM((3, OCC_WAYS * VIR_WAYS) + tile_shape, f32),
            dma((3,)), dma((ROWS // GROUP,)),
            dma((2,)), dma((2,)), dma((2,)), dma((2,)),
            dma((2,)), dma((2,)), dma((2,)), dma((2,)), dma((2,)), dma((2,)),
            dma((3,)), dma((3,)),
        ],
        compiler_params=pltpu.CompilerParams(
            collective_id=0, has_side_effects=True, vmem_limit_bytes=60 * 1024 * 1024
        ),
        cost_estimate=pl.CostEstimate(flops=200_000_000, bytes_accessed=3_000_000, transcendentals=0),
    )(
        start_block.transpose(1, 0, 2),
        factors.transpose(0, 2, 1, 3),
        eps_occ,
        eps_vir.reshape(1, LANES),
    )
    coefs, block = pl.pallas_call(
        finish,
        out_shape=(
            jax.ShapeDtypeStruct((4, NV, NV), f32),
            jax.ShapeDtypeStruct((ROWS,) + tile_shape, f32),
        ),
        in_specs=[vmem] * 2,
        out_specs=(vmem, vmem),
        compiler_params=pltpu.CompilerParams(vmem_limit_bytes=4 * 1024 * 1024),
        cost_estimate=pl.CostEstimate(flops=400_000, bytes_accessed=200_000, transcendentals=0),
    )(small, resid)
    return coefs, block.transpose(1, 0, 2)


def solution(mesh):
    placed = (P(None, "occ", "vir"), P(None, "aux", "occ", "vir"), P("occ"), P("vir"))
    return jax.shard_map(
        on_device,
        mesh=mesh,
        in_specs=placed,
        out_specs=(P(), P(None, "occ", "vir")),
        check_vma=False,
    )
```

```python
import jax
import jax.numpy as jnp
from jax import lax
from jax.experimental import pallas as pl
from jax.experimental.pallas import tpu as pltpu
from jax.sharding import PartitionSpec as P

OCC_WAYS, VIR_WAYS = 4, 4
NV, ROWS, LANES, DEPTH = 8, 20, 128, 256
PAIRS = 40960
TILES = ROWS + 1
NEAR, BLOCKS, Z, SHARE = 8, 4, 16, 3
OWNERS = TILES // SHARE
CHIPS = 8
GROUP = 4
MESH = pl.DeviceIdType.MESH
f32, bf16 = jnp.float32, jnp.bfloat16


def split(value):
    high = value.astype(bf16)
    low = (value - high.astype(f32)).astype(bf16)
    return jnp.concatenate([high, low], axis=0)


def merge(value):
    return value[:NV] + value[NV:]


def apply(matrix, value, first=0):
    total = matrix[:, first:first + 1] * value[0:1, :]
    for m in range(1, NV):
        total = total + matrix[:, first + m:first + m + 1] * value[m:m + 1, :]
    return total


def iotas():
    return (
        lax.broadcasted_iota(jnp.int32, (NV, LANES), 0),
        lax.broadcasted_iota(jnp.int32, (NV, LANES), 1),
    )


def factor(gram):
    row, lane = iotas()
    work = jnp.where(lane < NV, gram, jnp.where(lane == row + NV, 1.0, 0.0))
    scale = jnp.ones((NV, 1), f32)
    rows1 = lax.broadcasted_iota(jnp.int32, (NV, 1), 0)
    for k in range(NV):
        pivot = work[k:k + 1, k:k + 1]
        scale = jnp.where(rows1 == k, pivot, scale)
        if k < NV - 1:
            ratio = jnp.where(rows1 > k, work[:, k:k + 1] / pivot, 0.0)
            work = work - ratio * work[k:k + 1, :]
    return work * (1.0 / jnp.sqrt(scale))


def columns(sums):
    _, lane = iotas()
    out = jnp.zeros((NV, LANES), f32)
    for m, value in enumerate(sums):
        out = jnp.where(lane == m, jnp.sum(value, axis=1, keepdims=True), out)
    return out


def products(lefts, rights):
    sums = []
    for m in range(NV):
        total = lefts[0] * rights[0][m:m + 1, :]
        for left, right in zip(lefts[1:], rights[1:]):
            total = total + left * right[m:m + 1, :]
        sums.append(total)
    return sums


def kernel(
    start_hbm, fac_hbm, occ_hbm, vir_hbm,
    coef_ref, resid_ref,
    start, fac, eocc, evir, q1, q2, r1, xhat,
    cc, cm, part, rs, cx, ag, gm,
    in_sem, fac_sem, cc_send, cc_recv, cm_send, cm_recv,
    rs_send, rs_recv, cx_send, cx_recv, ag_send, ag_recv, g_send, g_recv,
):
    aux = lax.axis_index("aux")
    occ = lax.axis_index("occ")
    vir = lax.axis_index("vir")
    spot = occ * VIR_WAYS + vir
    core = lax.rem(vir, 2)
    chip = occ * 2 + vir // 2
    side = aux // Z
    block = lax.rem(aux, Z) // BLOCKS
    place = lax.rem(aux, BLOCKS)
    role = lax.rem(side * BLOCKS + place + BLOCKS * core, NEAR)
    owner = role < OWNERS
    own = pl.ds(role * SHARE, SHARE)

    def near(other):
        spot_of = lax.rem(other + BLOCKS * core, NEAR)
        return {"aux": (spot_of // BLOCKS) * Z + block * BLOCKS + lax.rem(spot_of, BLOCKS)}

    def far(d):
        return {"aux": side * Z + lax.rem(block + d, BLOCKS) * BLOCKS + place}

    def mate(d):
        other = lax.rem(spot + d, OCC_WAYS * VIR_WAYS)
        return {"occ": other // VIR_WAYS, "vir": lax.rem(other, VIR_WAYS)}

    peers = [near(lax.rem(role + d, NEAR)) for d in range(1, NEAR)]
    crosses = [far(d) for d in range(1, BLOCKS)]
    mates = [mate(d) for d in range(1, OCC_WAYS * VIR_WAYS)]

    loads = [
        pltpu.make_async_copy(start_hbm, start, in_sem.at[0]),
        pltpu.make_async_copy(occ_hbm, eocc, in_sem.at[1]),
        pltpu.make_async_copy(vir_hbm, evir, in_sem.at[2]),
    ]
    fac_loads = [
        pltpu.make_async_copy(
            fac_hbm.at[:, pl.ds(GROUP * c, GROUP)], fac.at[:, pl.ds(GROUP * c, GROUP)], fac_sem.at[c]
        )
        for c in range(ROWS // GROUP)
    ]
    for load in loads:
        load.start()

    barrier = pltpu.get_barrier_semaphore()

    greeted = crosses + peers + mates
    for index, device in enumerate(greeted):
        pl.semaphore_signal(barrier, inc=1, device_id=device, device_id_type=MESH)
        if index == len(crosses) - 1:
            for load in fac_loads:
                load.start()

    for load in loads:
        load.wait()

    def delta(i):
        return evir[...] - eocc[i]

    def contract(source, waits):
        sums = [None, None]
        for i in range(0, ROWS, 2):
            if waits and i % GROUP == 0:
                fac_loads[i // GROUP].wait()
            left = jnp.concatenate([split(source[i]), split(source[i + 1])], axis=1)
            for s in range(2):
                right = jnp.concatenate([fac[s, i], fac[s, i + 1]], axis=1)
                term = lax.dot_general(
                    left, right, (((1,), (1,)), ((), ())), preferred_element_type=f32
                )
                sums[s] = term if sums[s] is None else sums[s] + term
        return [merge(sums[s])[:, LANES * h:LANES * (h + 1)] for s in range(2) for h in range(2)]

    def wait_bytes(ref, sem):
        pltpu.make_async_copy(ref, ref, sem).wait()

    def sum_group(step, tiles, first, small_products):
        for index, value in enumerate(tiles):
            cc[step, core, index] = value
        if first:
            pl.semaphore_wait(barrier, len(greeted))
        send(
            cc.at[step, core], cc.at[step, core], (cc_send.at[step], cc_recv.at[step]),
            {"vir": vir + 1 - 2 * core},
        )
        hand_out(step, small_products())
        wait_bytes(cc.at[step, 0], cc_recv.at[step])
        for index in range(len(tiles)):
            cm[step, chip, index] = cc[step, 0, index] + cc[step, 1, index]
        for d in range(1, CHIPS):
            other = lax.rem(chip + d, CHIPS)
            send(
                cm.at[step, chip], cm.at[step, chip], (cm_send.at[step], cm_recv.at[step]),
                {"occ": other // 2, "vir": lax.rem(other, 2) * 2 + core},
            )
        wait_bytes(cm.at[step, pl.ds(0, CHIPS - 1)], cm_recv.at[step])
        out = []
        for index in range(len(tiles)):
            sums = [cm[step, j, index] for j in range(CHIPS)]
            while len(sums) > 1:
                sums = [a + b for a, b in zip(sums[0::2], sums[1::2])]
            out.append(sums[0])
        return out

    def hand_out(k, value):
        gm[k, spot] = value
        for device in mates:
            send(gm.at[k, spot], gm.at[k, spot], (g_send.at[k], g_recv.at[k]), device)

    def gather(k):
        wait_bytes(gm.at[k, pl.ds(0, len(mates))], g_recv.at[k])
        sums = [gm[k, j] for j in range(OCC_WAYS * VIR_WAYS)]
        while len(sums) > 1:
            sums = [a + b for a, b in zip(sums[0::2], sums[1::2])]
        return sums[0]

    def send(source, target, sems, device):
        pltpu.make_async_remote_copy(
            src_ref=source, dst_ref=target, send_sem=sems[0], recv_sem=sems[1],
            device_id=device, device_id_type=MESH,
        ).start()

    def scatter(step, first, last):
        for d in range(1, NEAR):
            other = lax.rem(role + d, NEAR)

            @pl.when(jnp.logical_and(other >= first, other < last))
            def _():
                send(
                    part.at[step, pl.ds(other * SHARE, SHARE)], rs.at[step, role],
                    (rs_send.at[step], rs_recv.at[step]), peers[d - 1],
                )

        @pl.when(jnp.logical_and(role >= first, role < last))
        def _():
            rs[step, role] = part[step, own]

    def back(step, sums):
        scaled = [
            split(jnp.concatenate([2.0 * sums[0], 2.0 * sums[1]], axis=1)),
            split(jnp.concatenate([-sums[2], -sums[3]], axis=1)),
        ]
        for i in range(0, ROWS, 2):
            both = None
            for s in range(2):
                right = jnp.concatenate([fac[s, i], fac[s, i + 1]], axis=1)
                term = lax.dot_general(
                    scaled[s], right, (((1,), (0,)), ((), ())), preferred_element_type=f32
                )
                both = term if both is None else both + term
            both = merge(both)
            part[step, i] = both[:, :LANES]
            part[step, i + 1] = both[:, LANES:]
            if i + 2 == 4 * SHARE:
                scatter(step, 0, 4)
        scatter(step, 4, OWNERS)

    def spread(step, lower, turned, extra):
        @pl.when(owner)
        def _():
            wait_bytes(rs.at[step, pl.ds(0, NEAR - 1)], rs_recv.at[step])
            sums = [rs[step, j] for j in range(NEAR)]
            while len(sums) > 1:
                sums = [a + b for a, b in zip(sums[0::2], sums[1::2])]
            cx[step, block] = sums[0]
            for d in range(1, BLOCKS):
                send(
                    cx.at[step, block], cx.at[step, block],
                    (cx_send.at[step], cx_recv.at[step]), crosses[d - 1],
                )
            wait_bytes(cx.at[step, pl.ds(0, BLOCKS - 1)], cx_recv.at[step])
            total = (cx[step, 0] + cx[step, 1]) + (cx[step, 2] + cx[step, 3])
            for k in range(SHARE - 1):
                ag[step, role * SHARE + k] = apply(lower, total[k], NV)
            last = role * SHARE + SHARE - 1

            @pl.when(role < OWNERS - 1)
            def _():
                ag[step, last] = apply(lower, total[SHARE - 1], NV)

            @pl.when(role == OWNERS - 1)
            def _():
                half = apply(lower, (total[SHARE - 1] + extra) * (1.0 / PAIRS), NV)
                whole = apply(half, turned)
                ag[step, last] = jnp.where(lane < NV, whole, half)

            for device in peers:
                send(
                    ag.at[step, own], ag.at[step, own],
                    (ag_send.at[step], ag_recv.at[step]), device,
                )
            wait_bytes(ag.at[step, pl.ds(0, TILES - SHARE)], ag_recv.at[step])

        @pl.when(jnp.logical_not(owner))
        def _():
            wait_bytes(ag.at[step], ag_recv.at[step])

    def small(left, right):
        return lax.dot_general(
            left, right, (((1,), (1,)), ((), ())),
            precision=lax.Precision.HIGHEST, preferred_element_type=f32,
        )

    def wide(value):
        return jnp.concatenate(
            [value, jnp.zeros((value.shape[0], LANES - value.shape[1]), f32)], axis=1
        )

    row, lane = iotas()
    weights = [2.0, 2.0, -1.0, -1.0]

    def turn(lower):
        return wide(small(jnp.where(lane == row, 1.0, 0.0)[:, :NV], lower[:, NV:2 * NV]))

    vecs = [start[i] for i in range(ROWS)]
    shifted = [vecs[i] * delta(i) for i in range(ROWS)]
    sums = sum_group(
        0, contract(vecs, True), True, lambda: columns(products(vecs, vecs) + products(vecs, shifted))
    )
    part[0, ROWS] = columns(products([w * v for w, v in zip(weights, sums)], sums))
    back(0, sums)
    grams = gather(0)
    lower = factor(grams * (1.0 / PAIRS))
    for index in range(4):
        xhat[index] = apply(lower, sums[index], NV)
    for i in range(ROWS):
        q1[i] = apply(lower, start[i], NV)
    extra = jnp.where(lane < NV, pltpu.roll(grams, LANES - NV, 1), 0.0)
    spread(0, lower, turn(lower), extra)
    proj = ag[0, ROWS]
    coef_ref[0] = proj
    for i in range(ROWS):
        r1[i] = ag[0, i] + delta(i) * q1[i] - apply(proj, q1[i])

    vecs = [r1[i] for i in range(ROWS)]
    moved = [delta(i) * q1[i] for i in range(ROWS)]
    shifted = [vecs[i] * delta(i) for i in range(ROWS)]
    sums = sum_group(
        1, contract(vecs, False), False,
        lambda: columns(products(vecs, vecs) + products(vecs, shifted) + products(vecs, moved)),
    )
    scaled = [w * v for w, v in zip(weights, sums)]
    part[1, ROWS] = columns(products(scaled, sums) + products(scaled, [xhat[k] for k in range(4)]))
    back(1, sums)
    grams = gather(1)
    lower = factor(grams * (1.0 / PAIRS))
    coef_ref[1] = jnp.where(lane >= row, lower, 0.0)
    for i in range(ROWS):
        q2[i] = apply(lower, r1[i], NV)
    extra = jnp.where(lane < 2 * NV, pltpu.roll(grams, LANES - NV, 1), 0.0)
    spread(1, lower, turn(lower), extra)
    proj = ag[1, ROWS]
    coef_ref[2] = proj
    for i in range(ROWS):
        resid_ref[i] = ag[1, i] + delta(i) * q2[i] - apply(proj, q2[i]) - apply(proj, q1[i], NV)

    vecs = [resid_ref[i] for i in range(ROWS)]
    hand_out(2, columns(products(vecs, vecs)))
    coef_ref[3] = gather(2) * (1.0 / PAIRS)

    for step in range(2):
        wait_bytes(cc.at[step, 0], cc_send.at[step])
        wait_bytes(cm.at[step, pl.ds(0, CHIPS - 1)], cm_send.at[step])

        @pl.when(owner)
        def _():
            wait_bytes(part.at[step, pl.ds(0, TILES - SHARE)], rs_send.at[step])
            wait_bytes(cx.at[step, pl.ds(0, BLOCKS - 1)], cx_send.at[step])
            wait_bytes(rs.at[step, pl.ds(0, NEAR - 1)], ag_send.at[step])

        @pl.when(jnp.logical_not(owner))
        def _():
            wait_bytes(part.at[step], rs_send.at[step])

    for k in range(3):
        wait_bytes(gm.at[k, pl.ds(0, len(mates))], g_send.at[k])


def finish(small_ref, resid_ref, coef_ref, next_ref):
    row, lane = iotas()
    lower = factor(small_ref[3])
    for k in range(3):
        coef_ref[k] = small_ref[k][:, :NV]
    coef_ref[3] = jnp.where(lane >= row, lower, 0.0)[:, :NV]
    for i in range(ROWS):
        next_ref[i] = apply(lower, resid_ref[i], NV)


def on_device(start_block, factors, eps_occ, eps_vir):
    tile_shape = (NV, LANES)
    dma = pltpu.SemaphoreType.DMA
    anywhere = pl.BlockSpec(memory_space=pltpu.MemorySpace.HBM)
    vmem = pl.BlockSpec(memory_space=pltpu.MemorySpace.VMEM)
    small, resid = pl.pallas_call(
        kernel,
        out_shape=(
            pltpu.VMEM((4,) + tile_shape, f32),
            pltpu.VMEM((ROWS,) + tile_shape, f32),
        ),
        in_specs=[anywhere] * 4,
        out_specs=(vmem, vmem),
        scratch_shapes=[
            pltpu.VMEM((ROWS,) + tile_shape, f32),
            pltpu.VMEM((2, ROWS, DEPTH, LANES), bf16),
            pltpu.SMEM((ROWS,), f32),
            pltpu.VMEM((1, LANES), f32),
            pltpu.VMEM((ROWS,) + tile_shape, f32),
            pltpu.VMEM((ROWS,) + tile_shape, f32),
            pltpu.VMEM((ROWS,) + tile_shape, f32),
            pltpu.VMEM((4,) + tile_shape, f32),
            pltpu.VMEM((2, 2, 4) + tile_shape, f32),
            pltpu.VMEM((2, CHIPS, 4) + tile_shape, f32),
            pltpu.VMEM((2, TILES) + tile_shape, f32),
            pltpu.VMEM((2, NEAR, SHARE) + tile_shape, f32),
            pltpu.VMEM((2, BLOCKS, SHARE) + tile_shape, f32),
            pltpu.VMEM((2, TILES) + tile_shape, f32),
            pltpu.VMEM((3, OCC_WAYS * VIR_WAYS) + tile_shape, f32),
            dma((3,)), dma((ROWS // GROUP,)),
            dma((2,)), dma((2,)), dma((2,)), dma((2,)),
            dma((2,)), dma((2,)), dma((2,)), dma((2,)), dma((2,)), dma((2,)),
            dma((3,)), dma((3,)),
        ],
        compiler_params=pltpu.CompilerParams(
            collective_id=0, has_side_effects=True, vmem_limit_bytes=60 * 1024 * 1024
        ),
        cost_estimate=pl.CostEstimate(flops=200_000_000, bytes_accessed=3_000_000, transcendentals=0),
    )(
        start_block.transpose(1, 0, 2),
        factors.transpose(0, 2, 1, 3),
        eps_occ,
        eps_vir.reshape(1, LANES),
    )
    coefs, block = pl.pallas_call(
        finish,
        out_shape=(
            jax.ShapeDtypeStruct((4, NV, NV), f32),
            jax.ShapeDtypeStruct((ROWS,) + tile_shape, f32),
        ),
        in_specs=[vmem] * 2,
        out_specs=(vmem, vmem),
        compiler_params=pltpu.CompilerParams(vmem_limit_bytes=4 * 1024 * 1024),
        cost_estimate=pl.CostEstimate(flops=400_000, bytes_accessed=200_000, transcendentals=0),
    )(small, resid)
    return coefs, block.transpose(1, 0, 2)


def solution(mesh):
    placed = (P(None, "occ", "vir"), P(None, "aux", "occ", "vir"), P("occ"), P("vir"))
    return jax.shard_map(
        on_device,
        mesh=mesh,
        in_specs=placed,
        out_specs=(P(), P(None, "occ", "vir")),
        check_vma=False,
    )
```
